256 devices in a mesh: win: 32 (over z, y_lo, core), tile: 8 (over y_hi, x).
Axes of the slice: x: 4, y: 4 (y_hi: 2, y_lo: 2; y = y_hi * 2 + y_lo), z: 8, core: 2. Of those that a mesh axis runs over, the one named last changes fastest.
Arguments:
- frames_in: bfloat16 [384, 16, 6, 640], P('win', 'tile'), may hold values from -30 to 30
- w_attn: bfloat16 [4, 640, 640], replicated, may hold values from -0.25 to 0.25
- conv_weight: bfloat16 [27, 320, 320], replicated, may hold values from -0.0625 to 0.0625
- fade: int32 [32, 4], P('win'), may hold values from 4 to 15, as said below
- grad_out: bfloat16 [384, 16, 6, 640], P('win', 'tile'), may hold values from -6 to 6
Outputs:
- grad_x: bfloat16 [384, 16, 6, 640], P('win', 'tile')
- grad_attn: float32 [1638400], P(('win', 'tile'))
- grad_conv: float32 [2764800], P(('win', 'tile'))
The draws below stay inside these ranges and needn't reach their ends.
Inputs may be any that keep to these rules, and one draw needn't show every extreme that they name: `fade`: each row falls strictly from first entry to last.
All inputs are finite; a program needn't handle non-finite values.
Results may differ from the reference program's by a relative error of at most 0.014.
The reference program's roundings to bfloat16 on the way count: a program that leaves them out, or rounds other values in their place, can miss the bound.
Values may be sent and summed in bfloat16 or wider, within the bound.
No kernel may reach another device: no remote copies, remote signals or barrier semaphores. Data moves between devices by JAX's collectives and lax.ppermute only.
A program may use at most 128 MiB of HBM per device.

```python
import math
import jax
import jax.numpy as jnp
from jax import lax

C = 640
HEADS = 10
CONV = 320
WIN_LEN = 16
STRIDE = 12
OVER = 4
COLS = 6
NF = 384
NR = 16
N_WIN = 32


def draw_frames_in(key, part):
    key = jax.random.fold_in(key, 11)
    first = jax.random.fold_in(key, 0)
    base = jnp.clip(jax.random.normal(first, (NF, NR, COLS, C), jnp.float32), -5.0, 5.0)
    return base.astype(jnp.bfloat16)


def draw_fade(key, part):
    key = jax.random.fold_in(key, 23)
    steps = jax.random.randint(key, (N_WIN, OVER), 1, 4)
    row_ids = jnp.arange(N_WIN, dtype=jnp.int32)[:, None]
    col_ids = jnp.arange(OVER, dtype=jnp.int32)[None, :]
    steps = jnp.where((row_ids == 0) & (col_ids == 0), 1, steps)
    steps = jnp.where(row_ids == N_WIN - 1, 3, steps)
    return (16 - jnp.cumsum(steps, axis=1)).astype(jnp.int32)


def level_of(own_key, extent, pieces, low, top_value):
    def one(position, shards_of):
        draws = jax.random.uniform(jax.random.fold_in(jax.random.fold_in(own_key, 6), position), (shards_of,), jnp.float32, low / len(pieces), top_value / len(pieces))
        return jnp.repeat(jnp.exp(draws), extent[position] // shards_of).reshape((-1,) + (1,) * (len(extent) - position - 1))

    factor_of = one(*pieces[0])
    for cut in pieces[1:]:
        factor_of = factor_of * one(*cut)
    return factor_of


def centred(rng, shape, deviation, reach, cuts=(), kind=jnp.bfloat16):
    entries = jax.random.normal(rng, shape, jnp.float32) * deviation
    if len(cuts) > 0:
        entries = level_of(rng, shape, cuts, -0.22, 0.18) * entries
    return jnp.clip(entries, min=-reach, max=reach).astype(kind)


def setup_inputs(seed: int = 0) -> dict:
    key_list = jax.random.split(jax.random.key(seed), 6)
    return {
        "frames_in": draw_frames_in(jax.random.fold_in(key_list[5], 71), 0),
        "w_attn": centred(key_list[1], (4, C, C), C ** -0.5, 0.25),
        "conv_weight": centred(key_list[2], (27, CONV, CONV), (27 * CONV) ** -0.5, 0.0625),
        "fade": draw_fade(jax.random.fold_in(key_list[5], 71), 0),
        "grad_out": centred(key_list[4], (NF, NR, COLS, C), 1.0, 6.0, ((0, 32), (1, 8))),
    }


def silu_parts(value):
    sig = jax.nn.sigmoid(value)
    return (value * sig, sig * (1.0 + value * (1.0 - sig)))

def attend(window, w_attn, valid):
    places = window.shape[1]
    count = window.shape[0] * places
    flat = window.reshape(count, C)
    shape4 = (window.shape[0], places, HEADS, C // HEADS)
    scale = (C // HEADS) ** (-0.5)
    query = jnp.dot(flat, w_attn[0], preferred_element_type=jnp.float32).astype(jnp.bfloat16).reshape(shape4)
    keys = jnp.dot(flat, w_attn[1], preferred_element_type=jnp.float32).astype(jnp.bfloat16).reshape(shape4)
    values = jnp.dot(flat, w_attn[2], preferred_element_type=jnp.float32).astype(jnp.bfloat16).reshape(shape4)
    scores = jnp.einsum('tphd,sphd->phts', query.astype(jnp.float32), keys.astype(jnp.float32)) * scale
    scores = jnp.where(valid[None, None, None, :], scores, -1e+30)
    peak = lax.optimization_barrier(jnp.max(scores, axis=-1, keepdims=True))
    expo = jnp.exp(scores - peak)
    probs = expo / lax.optimization_barrier(jnp.sum(expo, axis=-1, keepdims=True))
    probs_b = probs.astype(jnp.bfloat16)
    heads_out = jnp.einsum('phts,sphd->tphd', probs_b.astype(jnp.float32), values.astype(jnp.float32))
    heads_out = heads_out.astype(jnp.bfloat16).reshape(count, C)
    branch = jnp.dot(heads_out, w_attn[3], preferred_element_type=jnp.float32)
    return (flat, query, keys, values, probs, probs_b, heads_out, branch.reshape(window.shape[0], places, C))

def attend_back(window, w_attn, valid, grad_branch):
    flat, query, keys, values, probs, probs_b, heads_out, branch = attend(window, w_attn, valid)
    count = flat.shape[0]
    scale = (C // HEADS) ** (-0.5)
    gflat = grad_branch.reshape(count, C)
    grad_heads = jnp.dot(gflat, w_attn[3].T, preferred_element_type=jnp.float32).astype(jnp.bfloat16)
    sum_o = jnp.dot(heads_out.T, gflat, preferred_element_type=jnp.float32)
    gh4 = grad_heads.reshape(query.shape)
    grad_probs = jnp.einsum('tphd,sphd->phts', gh4.astype(jnp.float32), values.astype(jnp.float32))
    inner = lax.optimization_barrier(jnp.sum(probs * grad_probs, axis=-1, keepdims=True))
    grad_scores = (probs * (grad_probs - inner) * scale).astype(jnp.bfloat16).astype(jnp.float32)
    grad_q = jnp.einsum('phts,sphd->tphd', grad_scores, keys.astype(jnp.float32)).astype(jnp.bfloat16).reshape(count, C)
    grad_k = jnp.einsum('phts,tphd->sphd', grad_scores, query.astype(jnp.float32)).astype(jnp.bfloat16).reshape(count, C)
    grad_v = jnp.einsum('phts,tphd->sphd', probs_b.astype(jnp.float32), gh4.astype(jnp.float32)).astype(jnp.bfloat16).reshape(count, C)
    grad_window = jnp.dot(grad_q, w_attn[0].T, preferred_element_type=jnp.float32)
    grad_window = grad_window + jnp.dot(grad_k, w_attn[1].T, preferred_element_type=jnp.float32)
    grad_window = grad_window + jnp.dot(grad_v, w_attn[2].T, preferred_element_type=jnp.float32)
    sums = jnp.stack([jnp.dot(flat.T, grad_q, preferred_element_type=jnp.float32), jnp.dot(flat.T, grad_k, preferred_element_type=jnp.float32), jnp.dot(flat.T, grad_v, preferred_element_type=jnp.float32), sum_o])
    return (grad_window.reshape(window.shape[0], window.shape[1], C), sums)

def reference(frames_in, w_attn, conv_weight, fade, grad_out):
    places = NR * COLS
    main = frames_in.reshape(N_WIN, STRIDE, places, C)
    tail = jnp.concatenate([main[1:, :OVER], jnp.zeros((1, OVER, places, C), jnp.bfloat16)], 0)
    windows = jnp.concatenate([main, tail], 1)
    valid_all = (jnp.arange(WIN_LEN)[None, :] < STRIDE) | (jnp.arange(N_WIN)[:, None] < N_WIN - 1)
    branch_all = lax.map(lambda pair: attend(pair[0], w_attn, pair[1])[-1], (windows, valid_all))
    frac = fade.astype(jnp.float32) / 16.0
    prev = jnp.concatenate([jnp.zeros((1, OVER), jnp.float32), frac[:-1]], 0)
    head = 1.0 - prev
    beta = jnp.concatenate([head, jnp.ones((N_WIN, STRIDE - OVER), jnp.float32), frac], 1)
    carried = frac[:, :, None, None] * branch_all[:, STRIDE:]
    prev_carried = jnp.concatenate([jnp.zeros((1, OVER, places, C), jnp.float32), carried[:-1]], 0)
    own = jnp.concatenate([head[:, :, None, None] * branch_all[:, :OVER] + prev_carried, branch_all[:, OVER:STRIDE]], 1)
    mixed = frames_in.astype(jnp.float32) + own.reshape(NF, NR, COLS, C)
    act_f, slope = silu_parts(mixed[..., :CONV])
    act = act_f.astype(jnp.bfloat16)
    grad_c = grad_out[..., :CONV]
    pads = ((1, 1), (1, 1), (1, 1), (0, 0))
    act_pad = jnp.pad(act, pads)
    grad_pad = jnp.pad(grad_c, pads)
    cells = NF * NR * COLS
    conv_back = jnp.zeros((cells, CONV), jnp.float32)
    kernel = []
    grad_flat = grad_c.reshape(cells, CONV)
    for da in (-1, 0, 1):
        for db in (-1, 0, 1):
            for dc in (-1, 0, 1):
                tap = 9 * (da + 1) + 3 * (db + 1) + (dc + 1)
                ahead = act_pad[1 + da:1 + da + NF, 1 + db:1 + db + NR, 1 + dc:1 + dc + COLS].reshape(cells, CONV)
                behind = grad_pad[1 - da:1 - da + NF, 1 - db:1 - db + NR, 1 - dc:1 - dc + COLS].reshape(cells, CONV)
                conv_back = conv_back + jnp.dot(behind, conv_weight[tap].T, preferred_element_type=jnp.float32)
                kernel.append(jnp.dot(ahead.T, grad_flat, preferred_element_type=jnp.float32))
    extra = jnp.concatenate([conv_back.reshape(NF, NR, COLS, CONV) * slope, jnp.zeros((NF, NR, COLS, C - CONV), jnp.float32)], -1)
    grad_mixed = grad_out.astype(jnp.float32) + extra
    gmain = grad_mixed.reshape(N_WIN, STRIDE, places, C)
    gtail = jnp.concatenate([gmain[1:, :OVER], jnp.zeros((1, OVER, places, C), jnp.float32)], 0)
    grad_branch = (beta[:, :, None, None] * jnp.concatenate([gmain, gtail], 1)).astype(jnp.bfloat16)

    def step(total, items):
        window, valid, gb = items
        gw, sums = attend_back(window, w_attn, valid, gb)
        return (total + sums, gw)
    sums, grad_windows = lax.scan(step, jnp.zeros((4, C, C), jnp.float32), (windows, valid_all, grad_branch))
    back = jnp.concatenate([jnp.zeros((1, OVER, places, C), jnp.float32), grad_windows[:-1, STRIDE:]], 0)
    back = jnp.concatenate([back, jnp.zeros((N_WIN, STRIDE - OVER, places, C), jnp.float32)], 1)
    total = gmain + grad_windows[:, :STRIDE] + back
    grad_x = total.reshape(NF, NR, COLS, C).astype(jnp.bfloat16)
    factor = 1.0 / math.sqrt(NF * NR * COLS)
    return (grad_x, sums.reshape(-1) * factor, jnp.stack(kernel).reshape(-1) * factor)
```

```python
import functools
import math

import jax
import jax.numpy as jnp
from jax import lax
from jax.experimental import pallas as pl
from jax.experimental.pallas import tpu as pltpu
from jax.sharding import PartitionSpec as P

HEADS = 10
CONV = 320
WIN_LEN = 16
STRIDE = 12
OVER = 4
WIDTH = 640
PLACES = 16
OWN = STRIDE * PLACES
TAIL = OVER * PLACES
ALL = OWN + TAIL
SLOTS_C = 9
SLOTS_A = 5
SLOTS = SLOTS_C + SLOTS_A
SB = 32
F32 = jnp.float32
BF16 = jnp.bfloat16
ROWS_C = 27 * CONV

NN = (((1,), (0,)), ((), ()))
NT = (((1,), (1,)), ((), ()))
TN = (((0,), (0,)), ((), ()))


def dot(a, b, dims=NN):
    return lax.dot_general(a, b, dims, preferred_element_type=F32)


def call(kernel, outs, scratch=(), specs=None, out_specs=None, aliases=None, cost=None):
    if out_specs is None:
        out_specs = tuple(vm(len(outs))) if isinstance(outs, tuple) else vm(1)[0]
    return pl.pallas_call(
        kernel,
        out_shape=outs,
        in_specs=specs,
        out_specs=out_specs,
        scratch_shapes=scratch,
        input_output_aliases=aliases or {},
        compiler_params=pltpu.CompilerParams(vmem_limit_bytes=56 << 20),
        cost_estimate=cost,
    )


def vm(n):
    return [pl.BlockSpec(memory_space=pltpu.VMEM)] * n


def sm(n):
    return [pl.BlockSpec(memory_space=pltpu.SMEM)] * n


def shp(shape, dtype):
    return jax.ShapeDtypeStruct(shape, dtype)


def lane_half(rows):
    return lax.broadcasted_iota(jnp.int32, (rows, 128), 1) < 64


def forward_kernel(info, fade, own, tail, w, qkv, probs, heads, branch, carried):
    x = jnp.concatenate([own[...], tail[...]], 0)
    for k in range(3):
        qkv[:, WIDTH * k : WIDTH * (k + 1)] = dot(x, w[k]).astype(BF16)
    scale = 64 ** (-0.5)
    row = lax.broadcasted_iota(jnp.int32, (ALL, ALL), 0)
    col = lax.broadcasted_iota(jnp.int32, (ALL, ALL), 1)
    limit = ALL - TAIL * info[0]
    bias = jnp.where((((row ^ col) & (PLACES - 1)) == 0) & (col < limit), 0.0, -1e30)
    first = lane_half(ALL)
    for pair in range(HEADS // 2):
        at = 128 * pair
        q = qkv[:, at : at + 128]
        k = qkv[:, WIDTH + at : WIDTH + at + 128]
        v = qkv[:, 2 * WIDTH + at : 2 * WIDTH + at + 128]
        results = []
        for side in range(2):
            mine = jnp.where(first if side == 0 else ~first, q, jnp.zeros_like(q))
            scores = dot(mine, k, NT) * scale + bias
            expo = jnp.exp(scores - jnp.max(scores, axis=-1, keepdims=True))
            prob = expo * (1.0 / jnp.sum(expo, axis=-1, keepdims=True))
            probs[2 * pair + side] = prob
            results.append(dot(prob.astype(BF16), v))
        heads[:, at : at + 128] = jnp.where(first, results[0], results[1]).astype(BF16)
    out = dot(heads[...], w[3])
    branch[...] = out[:OWN]
    lines = lax.broadcasted_iota(jnp.int32, (16, WIDTH), 0)
    table = jnp.zeros((16, WIDTH), F32)
    for t in range(OVER):
        frac = fade[0, t].astype(F32) / 16.0
        part = out[OWN + PLACES * t : OWN + PLACES * (t + 1)]
        carried[PLACES * t : PLACES * (t + 1)] = (frac * part).astype(BF16)
        table = jnp.where(lines == t, frac, table)
    carried[TAIL:] = table.astype(BF16)


def shifted(g, c):
    if c == 1:
        return jnp.concatenate([g[-1:], g[:-1]], 0)
    if c == -1:
        return jnp.concatenate([g[1:], g[:1]], 0)
    return g


def slab_of(g, b, c):
    width = g.shape[-1]
    lines = shifted(g, c).reshape(STRIDE + 2, 32, width)
    lines = lines[:, 8 * (1 - b) : 8 * (1 - b) + 16, :]
    return lines.astype(BF16).reshape((STRIDE + 2) * 16, width)


def conv_back_kernel(g, w, out, slabs, acc):
    lines = g[...].astype(F32)
    for b in (-1, 0, 1):
        for c in (-1, 0, 1):
            slabs[3 * (b + 1) + c + 1] = slab_of(lines, b, c)
    for a in (-1, 0, 1):
        for j in range(9):
            part = slabs[j, 16 * (1 - a) : 16 * (1 - a) + OWN, :]
            term = dot(w[9 * (a + 1) + j], part, NT)
            if a == -1 and j == 0:
                acc[...] = term
            else:
                acc[...] += term
    out[...] = acc[...].T


def mixed_kernel(own, branch, before, back, gout, act, gmix, gown, gsend):
    lines = lax.broadcasted_iota(jnp.int32, (OWN, 1), 0)
    inside = (lines & 7) < 6
    prev = jnp.zeros((TAIL, 1), F32)
    for t in range(OVER):
        value = before[TAIL + t : TAIL + t + 1, 0:1].astype(F32)
        prev = jnp.where((lines[:TAIL] >> 4) == t, value, prev)
    head = 1.0 - prev
    top = head * branch[:TAIL] + before[:TAIL].astype(F32)
    mixed = own[...].astype(F32) + jnp.concatenate([top, branch[TAIL:]], 0)
    conv_in = mixed[:, :CONV]
    sig = 1.0 / (1.0 + jnp.exp(-conv_in))
    act[...] = (conv_in * sig).astype(BF16)
    slope = sig * (1.0 + conv_in * (1.0 - sig))
    extra = jnp.where(inside, back[...] * slope, 0.0)
    gmix[...] = gout[...].astype(F32)
    gmix[:, :CONV] += extra
    total = gmix[...]
    beta = jnp.concatenate([head, jnp.ones((OWN - TAIL, 1), F32)], 0)
    gown[...] = (beta * total).astype(BF16)
    gsend[...] = (prev * total[:TAIL]).astype(BF16)


def backward_kernel(info, qkv, probs, gown, gtail, w, gqkv, keep, send):
    scale = 64 ** (-0.5)
    gb = jnp.concatenate([gown[...], gtail[...]], 0)
    gh = dot(gb, w[3], NT).astype(BF16)
    first = lane_half(ALL)
    zero = jnp.zeros((ALL, 128), BF16)
    for pair in range(HEADS // 2):
        at = 128 * pair
        q = qkv[:, at : at + 128]
        k = qkv[:, WIDTH + at : WIDTH + at + 128]
        v = qkv[:, 2 * WIDTH + at : 2 * WIDTH + at + 128]
        g = gh[:, at : at + 128]
        results = []
        for side in range(2):
            prob = probs[2 * pair + side]
            gp = dot(jnp.where(first if side == 0 else ~first, g, zero), v, NT)
            inner = jnp.sum(prob * gp, axis=-1, keepdims=True)
            gs = (prob * (gp - inner) * scale).astype(BF16)
            results.append((dot(gs, k), dot(gs, q, TN), dot(prob.astype(BF16), g, TN)))
        for n in range(3):
            picked = jnp.where(first, results[0][n], results[1][n])
            gqkv[:, WIDTH * n + at : WIDTH * n + at + 128] = picked.astype(BF16)
    lower = info[1] == 0
    ends = []
    for n in range(4):
        part = gqkv[:, WIDTH * n : WIDTH * (n + 1)] if n < 3 else gb
        low, high = part[:, :256], part[:, 256:512]
        keep[:, 256 * n : 256 * (n + 1)] = jnp.where(lower, low, high)
        send[:, 256 * n : 256 * (n + 1)] = jnp.where(lower, high, low)
        ends.append(part[:, 512:])
    for n in range(2):
        one, two = ends[2 * n], ends[2 * n + 1]
        low = jnp.concatenate([one[:, :64], two[:, :64]], 1)
        high = jnp.concatenate([one[:, 64:], two[:, 64:]], 1)
        keep[:, 1024 + 128 * n : 1152 + 128 * n] = jnp.where(lower, low, high)
        send[:, 1024 + 128 * n : 1152 + 128 * n] = jnp.where(lower, high, low)


def window_kernel(gqkv, w, gmix, total, back):
    acc = dot(gqkv[:, :WIDTH], w[0], NT)
    acc += dot(gqkv[:, WIDTH : 2 * WIDTH], w[1], NT)
    acc += dot(gqkv[:, 2 * WIDTH :], w[2], NT)
    total[...] = gmix[...] + acc[:OWN]
    back[...] = acc[OWN:].astype(BF16)


def conv_sum_kernel(act1, act2, g1, g2, out, slabs, wide, narrow, stage, sem):
    for n, g in enumerate((g1, g2)):
        lines = g[...].astype(F32)
        for b in (-1, 0, 1):
            for c in (-1, 0, 1):
                slabs[n, 3 * (b + 1) + c + 1] = slab_of(lines, b, c)
    turned = jnp.concatenate([act1[...], act2[...]], 0).T
    wide[ROWS_C:, :] = jnp.zeros((16, 128), F32)
    narrow[...] = jnp.zeros(narrow.shape, F32)
    for a in (-1, 0, 1):
        for j in range(9):
            tap = 9 * (a + 1) + j
            rows = slice(16 * (1 - a), 16 * (1 - a) + OWN)
            both = jnp.concatenate([slabs[0, j, rows, :], slabs[1, j, rows, :]], 0)
            part = dot(turned, both)
            wide[CONV * tap : CONV * (tap + 1), :] = part[:, :128]
            for q in range(4):
                start = SB + CONV * tap - SLOTS_C * q
                narrow[start : start + CONV, 32 * q : 32 * (q + 1)] = part[:, 128:]
    for t in range(8):
        start = (135 * t) // 4
        for s in range(SLOTS_C):
            at = start + s
            parts = [wide[pl.ds(at + SLOTS_C * q, 32, stride=270), :] for q in range(4)]
            parts.append(narrow[pl.ds(SB + at, 32, stride=270), :])
            stage[t, s] = jnp.concatenate(parts, 1).astype(BF16)
    copy = pltpu.make_async_copy(stage, out.at[:, 0:SLOTS_C], sem)
    copy.start()
    copy.wait()


def attn_sum_kernel(a1, a2, b1, b2, held, out, sums, stage, sem):
    del held
    turned = jnp.concatenate([a1[...], a2[...]], 0).T
    b = jnp.concatenate([b1[...], b2[...]], 0)
    flat, heads = turned[:WIDTH], turned[WIDTH:]
    part = dot(flat, b[:, : 3 * 256])
    for n in range(6):
        sums[n][...] = part[:, 128 * n : 128 * (n + 1)]
    part = dot(heads, b[:, 3 * 256 : 4 * 256])
    for n in range(2):
        sums[6 + n][...] = part[:, 128 * n : 128 * (n + 1)]
    first = lane_half(WIDTH)
    sums[8][...] = dot(flat, b[:, 1024:1152])
    tail = b[:, 1152:]
    sums[9][...] = jnp.where(first, dot(flat, tail), dot(heads, tail))
    small = lane_half(8)
    for t in range(8):
        for e in range(SLOTS_A):
            one = pl.ds(10 * t + e, 8, stride=80)
            two = pl.ds(10 * t + e + SLOTS_A, 8, stride=80)
            lines = []
            for k in range(4):
                x, y = sums[8 + k // 2][one, :], sums[8 + k // 2][two, :]
                if k % 2 == 0:
                    last = jnp.where(small, x, pltpu.roll(y, 64, 1))
                else:
                    last = jnp.where(small, pltpu.roll(x, 64, 1), y)
                cells = [sums[2 * k + n][at, :] for at in (one, two) for n in range(2)]
                lines.append(jnp.concatenate(cells + [last], 1))
            stage[t, e] = jnp.concatenate(lines, 0).astype(BF16)
    copy = pltpu.make_async_copy(stage, out.at[:, SLOTS_C:SLOTS], sem)
    copy.start()
    copy.wait()


def gather_kernel(given, out, sums):
    for s in range(SLOTS):
        total = given[0, s].astype(F32)
        for n in range(1, 8):
            total += given[n, s].astype(F32)
        for n in range(5):
            sums[n][32 * s : 32 * (s + 1), :] = total[:, 128 * n : 128 * (n + 1)]
    for w in range(32):
        parts = [sums[n][pl.ds(w, SLOTS, stride=32), :] for n in range(5)]
        out[w] = jnp.concatenate(parts, 1).astype(BF16)


def passed_along(block, axis, distance):
    devices = range(lax.axis_size(axis))
    route = [(i - distance, i) for i in devices if i - distance in devices]
    return lax.ppermute(block, axis, route)


def swapped(block):
    return lax.ppermute(block, "win", [(i, i ^ 1) for i in range(lax.axis_size("win"))])


def extended(block, axis, dim):
    count = block.shape[dim]
    low = passed_along(lax.slice_in_dim(block, count - 1, None, axis=dim), axis, 1)
    high = passed_along(lax.slice_in_dim(block, 0, 1, axis=dim), axis, -1)
    return jnp.concatenate([low, block, high], axis=dim)


def local(frames_in, w_attn, conv_weight, fade, grad_out):
    position = lax.axis_index("win")
    core = position % 2
    last = (position == lax.axis_size("win") - 1).astype(jnp.int32)
    info = jnp.stack([last, core.astype(jnp.int32)])
    pad = ((0, 0), (0, 0), (0, 2), (0, 0))
    own = jnp.pad(frames_in, pad).reshape(OWN, WIDTH)
    tail = passed_along(own[:TAIL], "win", -1)
    gpad = jnp.pad(grad_out, pad)
    gout = gpad.reshape(OWN, WIDTH)
    ghalo = extended(extended(gpad[..., :CONV], "tile", 1), "win", 0)
    ghalo = ghalo.reshape((STRIDE + 2) * 32, CONV)
    glow, ghigh = ghalo[:, : CONV // 2], ghalo[:, CONV // 2 :]
    gkeep = jnp.where(core == 0, glow, ghigh)
    gother = swapped(jnp.where(core == 0, ghigh, glow))

    qkv, probs, heads, branch, carried = call(
        forward_kernel,
        (
            shp((ALL, 3 * WIDTH), BF16),
            shp((HEADS, ALL, ALL), F32),
            shp((ALL, WIDTH), BF16),
            shp((OWN, WIDTH), F32),
            shp((TAIL + 16, WIDTH), BF16),
        ),
        specs=sm(2) + vm(3),
    )(info, fade, own, tail, w_attn)
    before = passed_along(carried, "win", 1)
    mine = jnp.concatenate([jnp.concatenate([own, tail], 0), heads], 1)
    theirs = swapped(mine)
    back = call(
        conv_back_kernel,
        shp((OWN, CONV), F32),
        [pltpu.VMEM((9, 14 * 16, CONV), BF16), pltpu.VMEM((CONV, OWN), F32)],
        specs=vm(2),
    )(ghalo, conv_weight)
    act, gmix, gown, gsend = call(
        mixed_kernel,
        (
            shp((OWN, CONV), BF16),
            shp((OWN, WIDTH), F32),
            shp((OWN, WIDTH), BF16),
            shp((TAIL, WIDTH), BF16),
        ),
        specs=vm(5),
    )(own, branch, before, back, gout)
    gtail = passed_along(gsend, "win", -1)
    act_other = swapped(act)
    anyspace = pl.BlockSpec(memory_space=pl.ANY)
    shares = call(
        conv_sum_kernel,
        shp((8, SLOTS, 32, WIDTH), BF16),
        [
            pltpu.VMEM((2, 9, 14 * 16, CONV // 2), BF16),
            pltpu.VMEM((ROWS_C + 16, 128), F32),
            pltpu.VMEM((SB + ROWS_C + 32, 128), F32),
            pltpu.VMEM((8, SLOTS_C, 32, WIDTH), BF16),
            pltpu.SemaphoreType.DMA,
        ],
        specs=vm(4),
        out_specs=anyspace,
    )(act, act_other, gkeep, gother)
    gqkv, keep, send = call(
        backward_kernel,
        (shp((ALL, 3 * WIDTH), BF16), shp((ALL, 1280), BF16), shp((ALL, 1280), BF16)),
        specs=sm(1) + vm(5),
    )(info, qkv, probs, gown, gtail, w_attn)
    other = swapped(send)
    total, gback = call(
        window_kernel,
        (shp((OWN, WIDTH), F32), shp((TAIL, WIDTH), BF16)),
        specs=vm(3),
    )(gqkv, w_attn, gmix)
    returned = passed_along(gback, "win", 1)
    shares = call(
        attn_sum_kernel,
        shp((8, SLOTS, 32, WIDTH), BF16),
        [
            [pltpu.VMEM((WIDTH, 128), F32)] * 10,
            pltpu.VMEM((8, SLOTS_A, 32, WIDTH), BF16),
            pltpu.SemaphoreType.DMA,
        ],
        specs=vm(4) + [anyspace],
        out_specs=anyspace,
        aliases={4: 0},
    )(mine, theirs, keep, other, shares)
    shares = lax.all_to_all(shares, "tile", 0, 0, tiled=True)
    shares = call(
        gather_kernel,
        shp((32, SLOTS, WIDTH), BF16),
        [[pltpu.VMEM((32 * SLOTS, 128), F32)] * 5],
        specs=vm(1),
    )(shares)
    shares = lax.all_to_all(shares, "win", 0, 0, tiled=True)

    cells = STRIDE * 12 * lax.axis_size("win") * lax.axis_size("tile")
    factor = 1.0 / math.sqrt(cells)
    sums = jnp.sum(shares.reshape(16, 2, SLOTS, WIDTH).astype(F32), axis=0) * factor
    conv, attn = sums[:, :SLOTS_C], sums[:, SLOTS_C:]
    big = conv[..., :512].reshape(2, SLOTS_C, 4, 128)
    small = conv[..., 512:].reshape(2, SLOTS_C, 4, 32)
    conv = jnp.concatenate([big, small], -1).transpose(2, 1, 0, 3).reshape(-1)
    offset = 240 * lax.axis_index("tile") % 320
    grad_conv = lax.dynamic_slice(conv, (offset,), (10800,))
    big = attn[..., :512].reshape(2, SLOTS_A, 2, 256)
    small = attn[..., 512:].reshape(2, SLOTS_A, 2, 64)
    big = big.transpose(2, 1, 0, 3).reshape(10, 512)
    small = small.transpose(2, 1, 0, 3).reshape(10, 128)
    grad_attn = jnp.concatenate([big, small], -1).reshape(-1)

    total = jnp.concatenate([total[:TAIL] + returned.astype(F32), total[TAIL:]], 0)
    grad_x = total.astype(BF16).reshape(STRIDE, 2, 8, WIDTH)[:, :, :6]
    return (grad_x, grad_attn, grad_conv)


def solution(mesh):
    placed = (P("win", "tile", None, None), P(), P(), P("win", None), P("win", "tile", None, None))
    return jax.shard_map(
        local,
        mesh=mesh,
        in_specs=placed,
        out_specs=(P("win", "tile", None, None), P(("win", "tile")), P(("win", "tile"))),
        check_vma=False,
    )
```

```python
import functools
import math

import jax
import jax.numpy as jnp
from jax import lax
from jax.experimental import pallas as pl
from jax.experimental.pallas import tpu as pltpu
from jax.sharding import PartitionSpec as P

HEADS = 10
CONV = 320
WIN_LEN = 16
STRIDE = 12
OVER = 4
WIDTH = 640
PLACES = 16
OWN = STRIDE * PLACES
TAIL = OVER * PLACES
ALL = OWN + TAIL
SLOTS = 14
LINES = 240
GROUP = 4
QUARTER = CONV // GROUP
SHARED = (STRIDE + 2) * 16
SB = 8
F32 = jnp.float32
BF16 = jnp.bfloat16
ROWS_C = 27 * QUARTER

NN = (((1,), (0,)), ((), ()))
NT = (((1,), (1,)), ((), ()))
TN = (((0,), (0,)), ((), ()))


def dot(a, b, dims=NN):
    return lax.dot_general(a, b, dims, preferred_element_type=F32)


def call(kernel, outs, scratch=(), specs=None, out_specs=None, aliases=None, us=1.0):
    if out_specs is None:
        out_specs = tuple(vm(len(outs))) if isinstance(outs, tuple) else vm(1)[0]
    return pl.pallas_call(
        kernel,
        out_shape=outs,
        in_specs=specs,
        out_specs=out_specs,
        scratch_shapes=scratch,
        input_output_aliases=aliases or {},
        compiler_params=pltpu.CompilerParams(vmem_limit_bytes=28 << 20),
        cost_estimate=pl.CostEstimate(
            flops=int(us * 1e9), bytes_accessed=int(us * 3e6), transcendentals=0
        ),
    )


def vm(n):
    return [pl.BlockSpec(memory_space=pltpu.VMEM)] * n


def sm(n):
    return [pl.BlockSpec(memory_space=pltpu.SMEM)] * n


def shp(shape, dtype):
    return jax.ShapeDtypeStruct(shape, dtype)


def lane_half(rows):
    return lax.broadcasted_iota(jnp.int32, (rows, 128), 1) < 64


def forward_kernel(
    info, fade, own, tail, w, g0, g1, g2, g3, qkv, probs, mine, branch, carried, keep, send, edge
):
    lower = info[1] == 0
    row = (info[2] ^ (GROUP - 1)) * (1 - info[3]) + info[2] * info[3]
    border = jnp.zeros((SHARED, 384), BF16)
    for d, g in enumerate((g0, g1, g2, g3)):
        at = slice(SHARED * d, SHARED * (d + 1))
        left, right, end = g[:, :128], g[:, 128:256], g[:, 256:]
        keep[at, :128] = jnp.where(lower, left, right)
        send[at, :128] = jnp.where(lower, right, left)
        keep[at, 128:] = end
        send[at, 128:] = end
        border = jnp.where(row == d, g[...], border)
    border = border.astype(F32).reshape(STRIDE + 2, 16, 384)
    border = jnp.where(info[3] == 0, border[:, 8:], border[:, :8])
    edge[...] = border.reshape(SHARED // 2, 384).astype(BF16)
    x = jnp.concatenate([own[...], tail[:TAIL]], 0)
    mine[:, :WIDTH] = x
    for k in range(3):
        qkv[:, WIDTH * k : WIDTH * (k + 1)] = dot(x, w[k]).astype(BF16)
    scale = 64 ** (-0.5)
    row = lax.broadcasted_iota(jnp.int32, (ALL, ALL), 0)
    col = lax.broadcasted_iota(jnp.int32, (ALL, ALL), 1)
    limit = ALL - TAIL * info[0]
    bias = jnp.where((((row ^ col) & (PLACES - 1)) == 0) & (col < limit), 0.0, -1e30)
    first = lane_half(ALL)
    for pair in range(HEADS // 2):
        at = 128 * pair
        q = qkv[:, at : at + 128]
        k = qkv[:, WIDTH + at : WIDTH + at + 128]
        v = qkv[:, 2 * WIDTH + at : 2 * WIDTH + at + 128]
        results = []
        for side in range(2):
            picked = jnp.where(first if side == 0 else ~first, q, jnp.zeros_like(q))
            scores = dot(picked, k, NT) * scale + bias
            expo = jnp.exp(scores - jnp.max(scores, axis=-1, keepdims=True))
            prob = expo * (1.0 / jnp.sum(expo, axis=-1, keepdims=True))
            probs[2 * pair + side] = prob
            results.append(dot(prob.astype(BF16), v))
        mine[:, WIDTH + at : WIDTH + at + 128] = jnp.where(first, results[0], results[1]).astype(BF16)
    out = dot(mine[:, WIDTH:], w[3])
    branch[...] = out[:OWN]
    lines = lax.broadcasted_iota(jnp.int32, (16, WIDTH), 0)
    table = jnp.zeros((16, WIDTH), F32)
    for t in range(OVER):
        frac = fade[0, t].astype(F32) / 16.0
        part = out[OWN + PLACES * t : OWN + PLACES * (t + 1)]
        carried[PLACES * t : PLACES * (t + 1)] = (frac * part).astype(BF16)
        table = jnp.where(lines == t, frac, table)
    carried[TAIL:] = table.astype(BF16)


def shifted(g, c):
    if c == 1:
        return jnp.concatenate([g[-1:], g[:-1]], 0)
    if c == -1:
        return jnp.concatenate([g[1:], g[:1]], 0)
    return g


def slab_of(g, b, c, frames, rows):
    width = g.shape[-1]
    lines = shifted(g, c).reshape(frames, 8 * (rows + 2), width)
    lines = lines[:, 8 * (1 - b) : 8 * (1 - b) + 8 * rows, :]
    return lines.astype(BF16).reshape(frames * 8 * rows, width)


def conv_back_kernel(info, g0, g1, g2, g3, edge, w, out, send, slabs, acc):
    x, upper = info[2], info[3]
    lower = info[1] == 0
    border = edge[...].astype(F32).reshape(STRIDE + 2, 8, 384)
    start = jnp.where(lower, border[..., 128:256], border[..., :128])
    ends = jnp.concatenate([start, border[..., 256:]], -1)
    send[...] = ends.reshape(SHARED // 2, 256).astype(BF16)
    parts = [g[...].astype(F32).reshape(STRIDE + 2, 16, 384) for g in (g0, g1, g2, g3)]

    def row_of(n, half):
        return parts[n][:, 8 * half : 8 * half + 8]

    blank = jnp.zeros_like(border)
    low = jnp.where(x == 0, jnp.where(upper == 1, border, blank), row_of(1, 1))
    low = jnp.where(x == 2, row_of(3, 1), low)
    high = jnp.where(x == 3, jnp.where(upper == 1, blank, border), row_of(1, 0))
    high = jnp.where(x == 1, row_of(3, 0), high)
    lines = jnp.concatenate([low, parts[0], high], 1).reshape((STRIDE + 2) * 32, 384)
    lines = lines[:, :CONV]
    for b in (-1, 0, 1):
        for c in (-1, 0, 1):
            slabs[3 * (b + 1) + c + 1] = slab_of(lines, b, c, STRIDE + 2, 2)
    for a in (-1, 0, 1):
        for j in range(9):
            part = slabs[j, 16 * (1 - a) : 16 * (1 - a) + OWN, :]
            term = dot(w[9 * (a + 1) + j], part, NT)
            if a == -1 and j == 0:
                acc[...] = term
            else:
                acc[...] += term
    out[...] = acc[...].T


def mixed_kernel(info, own, branch, before, back, gout, act0, act1, act2, act3, gmix, gown, gsend):
    lines = lax.broadcasted_iota(jnp.int32, (OWN, 1), 0)
    inside = (lines & 7) < 6
    prev = jnp.zeros((TAIL, 1), F32)
    for t in range(OVER):
        value = before[TAIL + t : TAIL + t + 1, 0:1].astype(F32)
        prev = jnp.where((lines[:TAIL] >> 4) == t, value, prev)
    head = 1.0 - prev
    top = head * branch[:TAIL] + before[:TAIL].astype(F32)
    mixed = own[...].astype(F32) + jnp.concatenate([top, branch[TAIL:]], 0)
    conv_in = mixed[:, :CONV]
    sig = 1.0 / (1.0 + jnp.exp(-conv_in))
    value = (conv_in * sig).astype(BF16)
    channel = lax.broadcasted_iota(jnp.int32, (CONV, 128), 0)
    column = lax.broadcasted_iota(jnp.int32, (CONV, 128), 1)
    for d in range(GROUP):
        wanted = GROUP * column + (info[2] ^ d)
        pick = jnp.where((channel == wanted) & (column < QUARTER), 1.0, 0.0).astype(BF16)
        (act0, act1, act2, act3)[d][...] = dot(value, pick).astype(BF16)
    slope = sig * (1.0 + conv_in * (1.0 - sig))
    extra = jnp.where(inside, back[...] * slope, 0.0)
    gmix[...] = gout[...].astype(F32)
    gmix[:, :CONV] += extra
    total = gmix[...]
    beta = jnp.concatenate([head, jnp.ones((OWN - TAIL, 1), F32)], 0)
    gown[...] = (beta * total).astype(BF16)
    gsend[...] = (prev * total[:TAIL]).astype(BF16)


def backward_kernel(info, qkv, probs, gown, gtail, w, gqkv, keep, send):
    scale = 64 ** (-0.5)
    gb = jnp.concatenate([gown[...], gtail[...]], 0)
    gh = dot(gb, w[3], NT).astype(BF16)
    first = lane_half(ALL)
    zero = jnp.zeros((ALL, 128), BF16)
    for pair in range(HEADS // 2):
        at = 128 * pair
        q = qkv[:, at : at + 128]
        k = qkv[:, WIDTH + at : WIDTH + at + 128]
        v = qkv[:, 2 * WIDTH + at : 2 * WIDTH + at + 128]
        g = gh[:, at : at + 128]
        results = []
        for side in range(2):
            prob = probs[2 * pair + side]
            gp = dot(jnp.where(first if side == 0 else ~first, g, zero), v, NT)
            inner = jnp.sum(prob * gp, axis=-1, keepdims=True)
            gs = (prob * (gp - inner) * scale).astype(BF16)
            results.append((dot(gs, k), dot(gs, q, TN), dot(prob.astype(BF16), g, TN)))
        for n in range(3):
            picked = jnp.where(first, results[0][n], results[1][n])
            gqkv[:, WIDTH * n + at : WIDTH * n + at + 128] = picked.astype(BF16)
    lower = info[1] == 0
    ends = []
    for n in range(4):
        part = gqkv[:, WIDTH * n : WIDTH * (n + 1)] if n < 3 else gb
        low, high = part[:, :256], part[:, 256:512]
        keep[:, 256 * n : 256 * (n + 1)] = jnp.where(lower, low, high)
        send[:, 256 * n : 256 * (n + 1)] = jnp.where(lower, high, low)
        ends.append(part[:, 512:])
    for n in range(2):
        one, two = ends[2 * n], ends[2 * n + 1]
        low = jnp.concatenate([one[:, :64], two[:, :64]], 1)
        high = jnp.concatenate([one[:, 64:], two[:, 64:]], 1)
        keep[:, 1024 + 128 * n : 1152 + 128 * n] = jnp.where(lower, low, high)
        send[:, 1024 + 128 * n : 1152 + 128 * n] = jnp.where(lower, high, low)


def window_kernel(gqkv, w, gmix, total, back):
    acc = dot(gqkv[:, :WIDTH], w[0], NT)
    acc += dot(gqkv[:, WIDTH : 2 * WIDTH], w[1], NT)
    acc += dot(gqkv[:, 2 * WIDTH :], w[2], NT)
    total[...] = gmix[...] + acc[:OWN]
    back[...] = acc[OWN:].astype(BF16)


def by_row(pieces, x):
    rows = []
    for n in range(GROUP):
        low = jnp.where((x & 1) == 0, pieces[n], pieces[n ^ 1])
        high = jnp.where((x & 1) == 0, pieces[n ^ 2], pieces[n ^ 3])
        rows.append(jnp.where((x & 2) == 0, low, high).reshape(STRIDE, 1, 16, 128))
    return jnp.concatenate(rows, 1).reshape(STRIDE * 64, 128)


def conv_sum_kernel(info, a0, a1, a2, a3, b0, b1, b2, b3, g1, g2, e1, e2, out, wide, narrow, stage, sem):
    x, upper = info[2], info[3]
    frames = STRIDE + 2
    half = CONV // 2
    left = [[], [], []]
    lines = []
    gap = jnp.zeros((QUARTER, 64), BF16)
    for acts, g, e in (((a0, a1, a2, a3), g1, e1), ((b0, b1, b2, b3), g2, e2)):
        turned = by_row([p[...] for p in acts], x).T[:QUARTER]
        left[0] += [gap, gap, turned]
        left[1] += [gap, turned, gap]
        left[2] += [turned, gap, gap]

        def cut(value):
            value = value.astype(F32)
            end = value[:, 128:]
            end = jnp.where(info[1] == 0, end, pltpu.roll(end, 96, 1))[:, :32]
            return jnp.concatenate([value[:, :128], end], 1).reshape(frames, -1, half)

        border = cut(e[...])
        before = jnp.where(upper == 1, border, 0.0)
        after = jnp.where(upper == 1, 0.0, border)
        places = [pl.ds(pl.multiple_of(SHARED * (x ^ n), 16), SHARED) for n in range(GROUP)]
        inner = [cut(g[at, :]) for at in places]
        lines.append(jnp.concatenate([before] + inner + [after], 1).reshape(frames * 80, half))
    left = jnp.concatenate([jnp.concatenate(line, 1) for line in left], 0)
    wide[ROWS_C:, :] = jnp.zeros((16, 128), F32)
    narrow[...] = jnp.zeros(narrow.shape, F32)
    for b in (-1, 0, 1):
        for c in (-1, 0, 1):
            slabs = [slab_of(line, b, c, frames, 8) for line in lines]
            part = dot(left, jnp.concatenate(slabs, 0))
            for a in range(3):
                at = QUARTER * (9 * a + 3 * (b + 1) + c + 1)
                block = part[QUARTER * a : QUARTER * (a + 1)]
                wide[at : at + QUARTER, :] = block[:, :128]
                for q in range(4):
                    start = SB + at - q
                    narrow[start : start + QUARTER, 32 * q : 32 * (q + 1)] = block[:, 128:]
    lane = lax.broadcasted_iota(jnp.int32, (16, 128), 1)
    for t in range(8):
        starts = [(270 * p + (135 * t) // 4 - x + 3) >> 2 for p in range(2)]
        for p in range(2):
            for h in range(2):
                at = starts[p] + 4 * h
                parts = [wide[pl.ds(at + q, 16, stride=135), :] for q in range(4)]
                parts.append(narrow[pl.ds(SB + at, 16, stride=135), :])
                stage[t, 2 * p + h] = jnp.concatenate(parts, 1).astype(BF16)
        parts = [wide[pl.ds(starts[p] + 8, 16, stride=135), :] for p in range(2)]
        one = narrow[pl.ds(SB + starts[0] + 8, 16, stride=135), :]
        two = narrow[pl.ds(SB + starts[1] + 7, 16, stride=135), :]
        blank = jnp.zeros((16, 128), F32)
        parts += [blank, blank, jnp.where(lane < 32, one, two)]
        stage[t, 4] = jnp.concatenate(parts, 1).astype(BF16)
    copies = [
        pltpu.make_async_copy(stage.at[:, n], out.at[:, 16 * n : 16 * (n + 1)], sem.at[n])
        for n in range(5)
    ]
    for copy in copies:
        copy.start()
    for copy in copies:
        copy.wait()


def attn_sum_kernel(a1, a2, b1, b2, held, out, low, high, ends, stage, sem):
    del held
    turned = jnp.concatenate([a1[...], a2[...]], 0).T
    b = jnp.concatenate([b1[...], b2[...]], 0)
    flat, heads = turned[:WIDTH], turned[WIDTH:]
    part = dot(flat, b[:, : 3 * 256])
    for k in range(3):
        low[WIDTH * k : WIDTH * (k + 1), :] = part[:, 256 * k : 256 * k + 128]
        high[WIDTH * k : WIDTH * (k + 1), :] = part[:, 256 * k + 128 : 256 * (k + 1)]
    part = dot(heads, b[:, 3 * 256 : 4 * 256])
    low[3 * WIDTH :, :] = part[:, :128]
    high[3 * WIDTH :, :] = part[:, 128:]
    tail = b[:, 1152:]
    first = lane_half(WIDTH)
    pairs = (dot(flat, b[:, 1024:1152]), jnp.where(first, dot(flat, tail), dot(heads, tail)))
    for k in range(4):
        plain = pairs[k // 2]
        rolled = pltpu.roll(plain, 64, 1)
        here, there = (plain, rolled) if k % 2 == 0 else (rolled, plain)
        ends[SB + WIDTH * k : SB + WIDTH * (k + 1), :64] = here[:, :64]
        at = SB + WIDTH * k - 5
        ends[at : at + WIDTH, 64:] = there[:, 64:]
    for t in range(8):
        for e in range(5):
            halves = []
            for p in range(2):
                one = 80 * p + 10 * t + e
                rows = pl.ds(one, 16, stride=160)
                more = pl.ds(one + 5, 16, stride=160)
                last = ends[pl.ds(SB + one, 16, stride=160), :]
                parts = [low[rows, :], high[rows, :], low[more, :], high[more, :], last]
                halves.append(jnp.concatenate(parts, 1))
            stage[t, 32 * e : 32 * (e + 1)] = jnp.concatenate(halves, 0).astype(BF16)
    copy = pltpu.make_async_copy(stage, out.at[:, 80:LINES], sem)
    copy.start()
    copy.wait()


def gather_kernel(given, out, sums):
    def put(p, n, value):
        at = 16 * (SLOTS * p + n)
        for m in range(5):
            sums[m][at : at + 16, :] = value[:, 128 * m : 128 * (m + 1)]

    def read(n, at):
        return given[n, at : at + 16].astype(F32)

    lane = lax.broadcasted_iota(jnp.int32, (16, 128), 1)
    lasts = []
    for n in range(GROUP):
        for p in range(2):
            for h in range(2):
                at = 16 * (2 * p + h)
                put(p, 2 * n + h, read(n, at) + read(n + GROUP, at))
        lasts.append(read(n, 64) + read(n + GROUP, 64))
    for p in range(2):
        end = jnp.zeros((16, 128), F32)
        for n in range(GROUP):
            turn = (32 * (n - p)) % 128
            piece = lasts[n][:, 512:]
            if turn:
                piece = pltpu.roll(piece, turn, 1)
            end = jnp.where((lane >> 5) == n, piece, end)
        put(p, 8, jnp.concatenate([x[:, 128 * p : 128 * (p + 1)] for x in lasts] + [end], 1))
        for e in range(5):
            at = 80 + 32 * e + 16 * p
            total = read(0, at)
            for n in range(1, 8):
                total += read(n, at)
            put(p, 9 + e, total)
    for w in range(32):
        rows = pl.ds(16 * SLOTS * (w % 2) + w // 2, SLOTS, stride=16)
        out[w] = jnp.concatenate([sums[m][rows, :] for m in range(5)], 1).astype(BF16)


def passed_along(block, axis, distance):
    devices = range(lax.axis_size(axis))
    route = [(i - distance, i) for i in devices if i - distance in devices]
    return lax.ppermute(block, axis, route)


def swapped(block):
    return lax.ppermute(block, "win", [(i, i ^ 1) for i in range(lax.axis_size("win"))])


def exchanged(block, distance):
    return lax.ppermute(block, "tile", [(i, i ^ distance) for i in range(lax.axis_size("tile"))])


def local(frames_in, w_attn, conv_weight, fade, grad_out):
    position = lax.axis_index("win")
    tile = lax.axis_index("tile")
    core = position % 2
    last = position == lax.axis_size("win") - 1
    info = jnp.stack([last, core, tile % GROUP, tile // GROUP]).astype(jnp.int32)
    pad = ((0, 0), (0, 0), (0, 2), (0, 0))
    own = jnp.pad(frames_in, pad).reshape(OWN, WIDTH)
    gpad = jnp.pad(grad_out, pad)
    gout = gpad.reshape(OWN, WIDTH)
    gframes = jnp.pad(gpad[..., :CONV], ((0, 0), (0, 0), (0, 0), (0, 64)))
    gframes = gframes.reshape(OWN, 384)
    first = jnp.pad(gpad[0, ..., :CONV].reshape(16, CONV), ((0, 0), (0, CONV)))
    tail = passed_along(jnp.concatenate([own[:TAIL], first], 0), "win", -1)
    before = passed_along(gframes[OWN - 16 :], "win", 1)
    gframes = jnp.concatenate([before, gframes, tail[TAIL:, :384]], 0)
    pieces = [gframes] + [exchanged(gframes, d) for d in (1, 2, 3)]

    qkv, probs, mine, branch, carried, gkeep, gsend, gedge = call(
        forward_kernel,
        (
            shp((ALL, 3 * WIDTH), BF16),
            shp((HEADS, ALL, ALL), F32),
            shp((ALL, 2 * WIDTH), BF16),
            shp((OWN, WIDTH), F32),
            shp((TAIL + 16, WIDTH), BF16),
            shp((GROUP * SHARED, 256), BF16),
            shp((GROUP * SHARED, 256), BF16),
            shp((SHARED // 2, 384), BF16),
        ),
        specs=sm(2) + vm(7),
        us=4,
    )(info, fade, own, tail, w_attn, *pieces)
    gedge = exchanged(gedge, GROUP)
    before = passed_along(carried, "win", 1)
    theirs = swapped(mine)
    gother = swapped(gsend)
    back, esend = call(
        conv_back_kernel,
        (shp((OWN, CONV), F32), shp((SHARED // 2, 256), BF16)),
        [pltpu.VMEM((9, 14 * 16, CONV), BF16), pltpu.VMEM((CONV, OWN), F32)],
        specs=sm(1) + vm(6),
        us=3,
    )(info, *pieces, gedge, conv_weight)
    eother = swapped(esend)
    *acts, gmix, gown, gsend = call(
        mixed_kernel,
        (
            *[shp((OWN, 128), BF16)] * GROUP,
            shp((OWN, WIDTH), F32),
            shp((OWN, WIDTH), BF16),
            shp((TAIL, WIDTH), BF16),
        ),
        specs=sm(1) + vm(5),
        us=1,
    )(info, own, branch, before, back, gout)
    gtail = passed_along(gsend, "win", -1)
    acts = [acts[0]] + [exchanged(acts[d], d) for d in (1, 2, 3)]
    others = [swapped(act) for act in acts]
    ekeep = jnp.where(core == 0, gedge[:, :128], gedge[:, 128:256])
    ekeep = jnp.concatenate([ekeep, gedge[:, 256:]], -1)
    gqkv, keep, send = call(
        backward_kernel,
        (shp((ALL, 3 * WIDTH), BF16), shp((ALL, 1280), BF16), shp((ALL, 1280), BF16)),
        specs=sm(1) + vm(5),
        us=5,
    )(info, qkv, probs, gown, gtail, w_attn)
    other = swapped(send)
    total, gback = call(
        window_kernel,
        (shp((OWN, WIDTH), F32), shp((TAIL, WIDTH), BF16)),
        specs=vm(3),
        us=1,
    )(gqkv, w_attn, gmix)
    returned = passed_along(gback, "win", 1)
    anyspace = pl.BlockSpec(memory_space=pl.ANY)
    shares = call(
        conv_sum_kernel,
        shp((8, LINES, WIDTH), BF16),
        [
            pltpu.VMEM((ROWS_C + 16, 128), F32),
            pltpu.VMEM((SB + ROWS_C + 24, 128), F32),
            pltpu.VMEM((8, 5, 16, WIDTH), BF16),
            pltpu.SemaphoreType.DMA((5,)),
        ],
        specs=sm(1) + vm(12),
        out_specs=anyspace,
        us=4,
    )(info, *acts, *others, gkeep, gother, ekeep, eother)
    shares = call(
        attn_sum_kernel,
        shp((8, LINES, WIDTH), BF16),
        [
            pltpu.VMEM((4 * WIDTH, 128), F32),
            pltpu.VMEM((4 * WIDTH, 128), F32),
            pltpu.VMEM((SB + 4 * WIDTH, 128), F32),
            pltpu.VMEM((8, 160, WIDTH), BF16),
            pltpu.SemaphoreType.DMA,
        ],
        specs=vm(4) + [anyspace],
        out_specs=anyspace,
        aliases={4: 0},
        us=4,
    )(mine, theirs, keep, other, shares)
    shares = lax.all_to_all(shares, "tile", 0, 0, tiled=True)
    shares = call(
        gather_kernel,
        shp((32, SLOTS, WIDTH), BF16),
        [[pltpu.VMEM((32 * SLOTS, 128), F32)] * 5],
        specs=vm(1),
        us=1.5,
    )(shares)
    shares = lax.all_to_all(shares, "win", 0, 0, tiled=True)

    cells = STRIDE * 12 * lax.axis_size("win") * lax.axis_size("tile")
    factor = 1.0 / math.sqrt(cells)
    sums = jnp.sum(shares.reshape(16, 2, SLOTS, WIDTH).astype(F32), axis=0) * factor
    conv, attn = sums[:, :9], sums[:, 9:]
    big = conv[:, :8, :512].reshape(2, GROUP, 8, 128)
    last = conv[:, 8, :512].reshape(2, GROUP, 1, 128)
    big = jnp.concatenate([big, last], 2).transpose(1, 2, 0, 3).reshape(GROUP, 9, 256)
    small = conv[:, :8, 512:].reshape(2, GROUP, 8, 32)
    last = conv[:, 8, 512:].reshape(2, GROUP, 1, 32)
    small = jnp.concatenate([small, last], 2).transpose(1, 2, 0, 3).reshape(GROUP, 9, 64)
    conv = jnp.concatenate([big, small], -1)
    begin = (2 * position + (135 * tile) // 4) % GROUP
    conv = lax.dynamic_slice(jnp.concatenate([conv, conv], 0), (begin, 0, 0), (GROUP, 9, CONV))
    conv = conv.transpose(1, 0, 2).reshape(-1)
    grad_conv = lax.dynamic_slice(conv, (240 * tile % 320,), (10800,))
    big = attn[..., :512].reshape(2, 5, 2, 256)
    small = attn[..., 512:].reshape(2, 5, 2, 64)
    big = big.transpose(2, 1, 0, 3).reshape(10, 512)
    small = small.transpose(2, 1, 0, 3).reshape(10, 128)
    grad_attn = jnp.concatenate([big, small], -1).reshape(-1)

    total = jnp.concatenate([total[:TAIL] + returned.astype(F32), total[TAIL:]], 0)
    grad_x = total.astype(BF16).reshape(STRIDE, 2, 8, WIDTH)[:, :, :6]
    return (grad_x, grad_attn, grad_conv)


def solution(mesh):
    placed = (P("win", "tile", None, None), P(), P(), P("win", None), P("win", "tile", None, None))
    return jax.shard_map(
        local,
        mesh=mesh,
        in_specs=placed,
        out_specs=(P("win", "tile", None, None), P(("win", "tile")), P(("win", "tile"))),
        check_vma=False,
    )
```

```python
import functools
import math

import jax
import jax.numpy as jnp
from jax import lax
from jax.experimental import pallas as pl
from jax.experimental.pallas import tpu as pltpu
from jax.sharding import PartitionSpec as P

HEADS = 10
CONV = 320
WIN_LEN = 16
STRIDE = 12
OVER = 4
WIDTH = 640
PLACES = 16
OWN = STRIDE * PLACES
TAIL = OVER * PLACES
ALL = OWN + TAIL
UNIT = 12
BLOCKS = 38
ROUND = 8
TOTALS = 8 * UNIT + 2 * 25
GROUP = 4
QUARTER = CONV // GROUP
SHARED = (STRIDE + 2) * 16
SB = 8
F32 = jnp.float32
BF16 = jnp.bfloat16
ROWS_C = 27 * QUARTER

NN = (((1,), (0,)), ((), ()))
NT = (((1,), (1,)), ((), ()))
TN = (((0,), (0,)), ((), ()))


def dot(a, b, dims=NN):
    return lax.dot_general(a, b, dims, preferred_element_type=F32)


def call(kernel, outs, scratch=(), specs=None, out_specs=None, aliases=None, us=1.0):
    if out_specs is None:
        out_specs = tuple(vm(len(outs))) if isinstance(outs, tuple) else vm(1)[0]
    return pl.pallas_call(
        kernel,
        out_shape=outs,
        in_specs=specs,
        out_specs=out_specs,
        scratch_shapes=scratch,
        input_output_aliases=aliases or {},
        compiler_params=pltpu.CompilerParams(vmem_limit_bytes=16 << 20),
        cost_estimate=pl.CostEstimate(
            flops=int(us * 1e9), bytes_accessed=int(us * 3e6), transcendentals=0
        ),
    )


def vm(n):
    return [pl.BlockSpec(memory_space=pltpu.VMEM)] * n


def sm(n):
    return [pl.BlockSpec(memory_space=pltpu.SMEM)] * n


def shp(shape, dtype):
    return jax.ShapeDtypeStruct(shape, dtype)


def lane_half(rows):
    return lax.broadcasted_iota(jnp.int32, (rows, 128), 1) < 64


def spread(block):
    value = block.astype(F32)
    blank = jnp.zeros((value.shape[0], 2, value.shape[2]), F32)
    value = jnp.concatenate([value, blank], 1)
    return value.reshape(value.shape[0] * 8, value.shape[2]).astype(BF16)


def prepare_kernel(frames, cotangent, own, ahead, gout, gframes, last):
    own[...] = spread(frames[...])
    ahead[:TAIL] = own[:TAIL]
    value = spread(cotangent[...])
    gout[...] = value
    gframes[:, :CONV] = value[:, :CONV]
    gframes[:, CONV:] = jnp.zeros((OWN, 384 - CONV), BF16)
    ahead[TAIL:, :384] = gframes[:16]
    ahead[TAIL:, 384:] = jnp.zeros((16, WIDTH - 384), BF16)
    last[...] = gframes[OWN - 16 :]


def forward_kernel(info, fade, own, tail, w, qkv, probs, mine, branch, carried):
    x = jnp.concatenate([own[...], tail[:TAIL]], 0)
    mine[:, :WIDTH] = x
    for k in range(3):
        qkv[:, WIDTH * k : WIDTH * (k + 1)] = dot(x, w[k]).astype(BF16)
    scale = 64 ** (-0.5)
    row = lax.broadcasted_iota(jnp.int32, (ALL, ALL), 0)
    col = lax.broadcasted_iota(jnp.int32, (ALL, ALL), 1)
    limit = ALL - TAIL * info[0]
    bias = jnp.where((((row ^ col) & (PLACES - 1)) == 0) & (col < limit), 0.0, -1e30)
    first = lane_half(ALL)
    for pair in range(HEADS // 2):
        at = 128 * pair
        q = qkv[:, at : at + 128]
        k = qkv[:, WIDTH + at : WIDTH + at + 128]
        v = qkv[:, 2 * WIDTH + at : 2 * WIDTH + at + 128]
        results = []
        for side in range(2):
            picked = jnp.where(first if side == 0 else ~first, q, jnp.zeros_like(q))
            scores = dot(picked, k, NT) * scale + bias
            expo = jnp.exp(scores - jnp.max(scores, axis=-1, keepdims=True))
            prob = expo * (1.0 / jnp.sum(expo, axis=-1, keepdims=True))
            probs[2 * pair + side] = prob
            results.append(dot(prob.astype(BF16), v))
        mine[:, WIDTH + at : WIDTH + at + 128] = jnp.where(first, results[0], results[1]).astype(BF16)
    out = dot(mine[:, WIDTH:], w[3])
    branch[...] = out[:OWN]
    lines = lax.broadcasted_iota(jnp.int32, (16, WIDTH), 0)
    table = jnp.zeros((16, WIDTH), F32)
    for t in range(OVER):
        frac = fade[0, t].astype(F32) / 16.0
        part = out[OWN + PLACES * t : OWN + PLACES * (t + 1)]
        carried[PLACES * t : PLACES * (t + 1)] = (frac * part).astype(BF16)
        table = jnp.where(lines == t, frac, table)
    carried[TAIL:] = table.astype(BF16)


def shifted(g, c):
    if c == 1:
        return jnp.concatenate([g[-1:], g[:-1]], 0)
    if c == -1:
        return jnp.concatenate([g[1:], g[:1]], 0)
    return g


def slab_of(g, b, c, frames, rows):
    width = g.shape[-1]
    lines = shifted(g, c).reshape(frames, 8 * (rows + 2), width)
    lines = lines[:, 8 * (1 - b) : 8 * (1 - b) + 8 * rows, :]
    return lines.astype(BF16).reshape(frames * 8 * rows, width)


def conv_back_kernel(info, g0, g1, g2, g3, edge, w, out, keep, send, away, slabs, acc):
    x, upper = info[2], info[3]
    lower = info[1] == 0
    row = (x ^ (GROUP - 1)) * (1 - upper) + x * upper
    border = jnp.zeros((SHARED, 384), BF16)
    for d, g in enumerate((g0, g1, g2, g3)):
        at = slice(SHARED * d, SHARED * (d + 1))
        left, right, end = g[:, :128], g[:, 128:256], g[:, 256:]
        keep[at, :128] = jnp.where(lower, left, right)
        send[at, :128] = jnp.where(lower, right, left)
        keep[at, 128:] = end
        send[at, 128:] = end
        border = jnp.where(row == d, g[...], border)
    border = border.astype(F32).reshape(STRIDE + 2, 16, 384)
    border = jnp.where(upper == 0, border[:, 8:], border[:, :8])
    away[...] = border.reshape(SHARED // 2, 384).astype(BF16)
    border = edge[...].astype(F32).reshape(STRIDE + 2, 8, 384)
    parts = [g[...].astype(F32).reshape(STRIDE + 2, 16, 384) for g in (g0, g1, g2, g3)]

    def row_of(n, half):
        return parts[n][:, 8 * half : 8 * half + 8]

    blank = jnp.zeros_like(border)
    low = jnp.where(x == 0, jnp.where(upper == 1, border, blank), row_of(1, 1))
    low = jnp.where(x == 2, row_of(3, 1), low)
    high = jnp.where(x == 3, jnp.where(upper == 1, blank, border), row_of(1, 0))
    high = jnp.where(x == 1, row_of(3, 0), high)
    lines = jnp.concatenate([low, parts[0], high], 1).reshape((STRIDE + 2) * 32, 384)
    lines = lines[:, :CONV]
    for b in (-1, 0, 1):
        for c in (-1, 0, 1):
            slabs[3 * (b + 1) + c + 1] = slab_of(lines, b, c, STRIDE + 2, 2)
    for a in (-1, 0, 1):
        for j in range(9):
            part = slabs[j, 16 * (1 - a) : 16 * (1 - a) + OWN, :]
            term = dot(w[9 * (a + 1) + j], part, NT)
            if a == -1 and j == 0:
                acc[...] = term
            else:
                acc[...] += term
    out[...] = acc[...].T


def mixed_kernel(
    info, own, branch, before, back, gout, act0, act1, act2, act3, gmix, gown, gsend
):
    lines = lax.broadcasted_iota(jnp.int32, (OWN, 1), 0)
    inside = (lines & 7) < 6
    prev = jnp.zeros((TAIL, 1), F32)
    for t in range(OVER):
        value = before[TAIL + t : TAIL + t + 1, 0:1].astype(F32)
        prev = jnp.where((lines[:TAIL] >> 4) == t, value, prev)
    head = 1.0 - prev
    top = head * branch[:TAIL] + before[:TAIL].astype(F32)
    mixed = own[...].astype(F32) + jnp.concatenate([top, branch[TAIL:]], 0)
    conv_in = mixed[:, :CONV]
    sig = 1.0 / (1.0 + jnp.exp(-conv_in))
    value = (conv_in * sig).astype(BF16)
    channel = lax.broadcasted_iota(jnp.int32, (CONV, 128), 0)
    column = lax.broadcasted_iota(jnp.int32, (CONV, 128), 1)
    for d in range(GROUP):
        wanted = GROUP * column + (info[2] ^ d)
        pick = jnp.where((channel == wanted) & (column < QUARTER), 1.0, 0.0).astype(BF16)
        (act0, act1, act2, act3)[d][...] = dot(value, pick).astype(BF16)
    slope = sig * (1.0 + conv_in * (1.0 - sig))
    extra = jnp.where(inside, back[...] * slope, 0.0)
    gmix[...] = gout[...].astype(F32)
    gmix[:, :CONV] += extra
    total = gmix[...]
    beta = jnp.concatenate([head, jnp.ones((OWN - TAIL, 1), F32)], 0)
    gown[...] = (beta * total).astype(BF16)
    gsend[...] = (prev * total[:TAIL]).astype(BF16)


def backward_kernel(info, qkv, probs, gown, gtail, w, gqkv, keep, send):
    scale = 64 ** (-0.5)
    gb = jnp.concatenate([gown[...], gtail[...]], 0)
    gh = dot(gb, w[3], NT).astype(BF16)
    first = lane_half(ALL)
    zero = jnp.zeros((ALL, 128), BF16)
    for pair in range(HEADS // 2):
        at = 128 * pair
        q = qkv[:, at : at + 128]
        k = qkv[:, WIDTH + at : WIDTH + at + 128]
        v = qkv[:, 2 * WIDTH + at : 2 * WIDTH + at + 128]
        g = gh[:, at : at + 128]
        results = []
        for side in range(2):
            prob = probs[2 * pair + side]
            gp = dot(jnp.where(first if side == 0 else ~first, g, zero), v, NT)
            inner = jnp.sum(prob * gp, axis=-1, keepdims=True)
            gs = (prob * (gp - inner) * scale).astype(BF16)
            results.append((dot(gs, k), dot(gs, q, TN), dot(prob.astype(BF16), g, TN)))
        for n in range(3):
            picked = jnp.where(first, results[0][n], results[1][n])
            gqkv[:, WIDTH * n + at : WIDTH * n + at + 128] = picked.astype(BF16)
    lower = info[1] == 0
    ends = []
    for n in range(4):
        part = gqkv[:, WIDTH * n : WIDTH * (n + 1)] if n < 3 else gb
        low, high = part[:, :256], part[:, 256:512]
        keep[:, 256 * n : 256 * (n + 1)] = jnp.where(lower, low, high)
        send[:, 256 * n : 256 * (n + 1)] = jnp.where(lower, high, low)
        ends.append(part[:, 512:])
    for n in range(2):
        one, two = ends[2 * n], ends[2 * n + 1]
        low = jnp.concatenate([one[:, :64], two[:, :64]], 1)
        high = jnp.concatenate([one[:, 64:], two[:, 64:]], 1)
        keep[:, 1024 + 128 * n : 1152 + 128 * n] = jnp.where(lower, low, high)
        send[:, 1024 + 128 * n : 1152 + 128 * n] = jnp.where(lower, high, low)


def window_kernel(gqkv, w, gmix, total, back):
    acc = dot(gqkv[:, :WIDTH], w[0], NT)
    acc += dot(gqkv[:, WIDTH : 2 * WIDTH], w[1], NT)
    acc += dot(gqkv[:, 2 * WIDTH :], w[2], NT)
    total[...] = gmix[...] + acc[:OWN]
    back[...] = acc[OWN:].astype(BF16)


def conv_sum_kernel(info, a1, a2, g1, g2, e1, e2, out, wide, narrow, stage, sem):
    x, upper = info[2], info[3]
    frames = STRIDE + 2
    half = CONV // 2
    left = [[], [], []]
    lines = []
    gap = jnp.zeros((QUARTER, 64), BF16)
    for act, g, e in ((a1, g1, e1), (a2, g2, e2)):
        places = [pl.ds(pl.multiple_of(OWN * (x ^ n), 16), OWN) for n in range(GROUP)]
        rows = [act[at, :].reshape(STRIDE, 1, 16, 128) for at in places]
        turned = jnp.concatenate(rows, 1).reshape(STRIDE * 64, 128).T[:QUARTER]
        left[0] += [gap, gap, turned]
        left[1] += [gap, turned, gap]
        left[2] += [turned, gap, gap]

        def cut(value):
            value = value.astype(F32)
            end = value[:, 128:]
            end = jnp.where(info[1] == 0, end, pltpu.roll(end, 96, 1))[:, :32]
            return jnp.concatenate([value[:, :128], end], 1).reshape(frames, -1, half)

        border = e[...]
        start = jnp.where(info[1] == 0, border[:, :128], border[:, 128:256])
        border = cut(jnp.concatenate([start, border[:, 256:]], 1))
        before = jnp.where(upper == 1, border, 0.0)
        after = jnp.where(upper == 1, 0.0, border)
        places = [pl.ds(pl.multiple_of(SHARED * (x ^ n), 16), SHARED) for n in range(GROUP)]
        inner = [cut(g[at, :]) for at in places]
        lines.append(jnp.concatenate([before] + inner + [after], 1).reshape(frames * 80, half))
    left = jnp.concatenate([jnp.concatenate(line, 1) for line in left], 0)
    wide[ROWS_C:, :] = jnp.zeros((16, 128), F32)
    narrow[...] = jnp.zeros(narrow.shape, F32)
    for b in (-1, 0, 1):
        for c in (-1, 0, 1):
            slabs = [slab_of(line, b, c, frames, 8) for line in lines]
            part = dot(left, jnp.concatenate(slabs, 0))
            for a in range(3):
                at = QUARTER * (9 * a + 3 * (b + 1) + c + 1)
                block = part[QUARTER * a : QUARTER * (a + 1)]
                wide[at : at + QUARTER, :] = block[:, :128]
                for q in range(4):
                    start = SB + at - q
                    narrow[start : start + QUARTER, 32 * q : 32 * (q + 1)] = block[:, 128:]
    for t in range(8):
        for p in range(2):
            start = (270 * p + (135 * t) // 4 - x + 3) >> 2
            for y in range(2):
                blocks = []
                for n in range(UNIT):
                    if n < 9:
                        rows = pl.ds(start + 135 * y + n, ROUND, stride=270)
                        blocks.append(wide[rows, :])
                    else:
                        rows = pl.ds(SB + start + 135 * y + 4 * (n - 9), ROUND, stride=270)
                        blocks.append(narrow[rows, :])
                share = 8 * (2 * y + p) + t
                for n in range(0, UNIT, 2):
                    pair = jnp.concatenate(blocks[n : n + 2], 0).astype(BF16)
                    stage[share, 8 * n : 8 * n + 16] = pair
    copy = pltpu.make_async_copy(stage, out.at[:, 0 : 8 * UNIT], sem)
    copy.start()
    copy.wait()


def attn_sum_kernel(a1, a2, b1, b2, held, out, low, high, ends, stage, sem):
    del held
    turned = jnp.concatenate([a1[...], a2[...]], 0).T
    b = jnp.concatenate([b1[...], b2[...]], 0)
    flat, heads = turned[:WIDTH], turned[WIDTH:]
    part = dot(flat, b[:, : 3 * 256])
    for k in range(3):
        low[WIDTH * k : WIDTH * (k + 1), :] = part[:, 256 * k : 256 * k + 128]
        high[WIDTH * k : WIDTH * (k + 1), :] = part[:, 256 * k + 128 : 256 * (k + 1)]
    part = dot(heads, b[:, 3 * 256 : 4 * 256])
    low[3 * WIDTH :, :] = part[:, :128]
    high[3 * WIDTH :, :] = part[:, 128:]
    tail = b[:, 1152:]
    first = lane_half(WIDTH)
    pairs = (dot(flat, b[:, 1024:1152]), jnp.where(first, dot(flat, tail), dot(heads, tail)))
    for k in range(4):
        plain = pairs[k // 2]
        rolled = pltpu.roll(plain, 64, 1)
        here, there = (plain, rolled) if k % 2 == 0 else (rolled, plain)
        ends[SB + WIDTH * k : SB + WIDTH * (k + 1), :64] = here[:, :64]
        at = SB + WIDTH * k - 5
        ends[at : at + WIDTH, 64:] = there[:, 64:]
    for share in range(32):
        blocks = []
        for e in range(5):
            one = 80 * (share // 8) + 10 * (share % 8) + e
            rows = pl.ds(one, ROUND, stride=320)
            more = pl.ds(one + 5, ROUND, stride=320)
            blocks += [low[rows, :], high[rows, :], low[more, :], high[more, :]]
            blocks.append(ends[pl.ds(SB + one, ROUND, stride=320), :])
        blocks.append(jnp.zeros((ROUND, 128), F32))
        for n in range(0, 26, 2):
            pair = jnp.concatenate(blocks[n : n + 2], 0).astype(BF16)
            stage[share, 8 * n : 8 * n + 16] = pair
    copy = pltpu.make_async_copy(stage, out.at[:, 8 * UNIT :], sem)
    copy.start()
    copy.wait()


def gather_kernel(given, out, sums):
    def added(sources, rows):
        total = given[sources[0], rows].astype(F32)
        for n in sources[1:]:
            total += given[n, rows].astype(F32)
        return total

    count = 8 * UNIT
    for c in range(2):
        for n in range(GROUP):
            sources = [8 * (2 * y + c) + GROUP * h + n for y in range(2) for h in range(2)]
            at = count * (GROUP * c + n)
            sums[at : at + count, :] = added(sources, slice(0, count))
        sources = [8 * (2 * y + c) + t for y in range(2) for t in range(8)]
        at = 8 * (count + 25 * c)
        sums[at : at + 200, :] = added(sources, slice(count, count + 208))[:200]
    sums[8 * TOTALS :, :] = jnp.zeros((48, 128), F32)
    for z in range(ROUND):
        out[z] = sums[pl.ds(z, TOTALS + 6, stride=8), :].astype(BF16)


def passed_along(block, axis, distance):
    devices = range(lax.axis_size(axis))
    route = [(i - distance, i) for i in devices if i - distance in devices]
    return lax.ppermute(block, axis, route)


def swapped(block):
    return lax.ppermute(block, "win", [(i, i ^ 1) for i in range(lax.axis_size("win"))])


def exchanged(block, distance):
    return lax.ppermute(block, "tile", [(i, i ^ distance) for i in range(lax.axis_size("tile"))])


def local(frames_in, w_attn, conv_weight, fade, grad_out):
    position = lax.axis_index("win")
    tile = lax.axis_index("tile")
    core = position % 2
    last = position == lax.axis_size("win") - 1
    info = jnp.stack([last, core, tile % GROUP, tile // GROUP]).astype(jnp.int32)
    own, ahead, gout, gframes, glast = call(
        prepare_kernel,
        (
            shp((OWN, WIDTH), BF16),
            shp((TAIL + 16, WIDTH), BF16),
            shp((OWN, WIDTH), BF16),
            shp((OWN, 384), BF16),
            shp((16, 384), BF16),
        ),
        specs=vm(2),
    )(frames_in.reshape(2 * STRIDE, 6, WIDTH), grad_out.reshape(2 * STRIDE, 6, WIDTH))
    tail = passed_along(ahead, "win", -1)
    before = passed_along(glast, "win", 1)
    gframes = jnp.concatenate([before, gframes, tail[TAIL:, :384]], 0)
    pieces = [gframes] + [exchanged(gframes, d) for d in (1, 2, 3)]
    sides = gframes.reshape(STRIDE + 2, 2, 8, 384)
    sides = jnp.where(tile < GROUP, sides[:, 1], sides[:, 0]).reshape(SHARED // 2, 384)
    border = lax.ppermute(sides, "tile", [(GROUP - 1, GROUP), (GROUP, GROUP - 1)])

    qkv, probs, mine, branch, carried = call(
        forward_kernel,
        (
            shp((ALL, 3 * WIDTH), BF16),
            shp((HEADS, ALL, ALL), F32),
            shp((ALL, 2 * WIDTH), BF16),
            shp((OWN, WIDTH), F32),
            shp((TAIL + 16, WIDTH), BF16),
        ),
        specs=sm(2) + vm(3),
        us=4,
    )(info, fade, own, tail, w_attn)
    before = passed_along(carried, "win", 1)
    theirs = swapped(mine)
    back, gkeep, gaway, gedge = call(
        conv_back_kernel,
        (
            shp((OWN, CONV), F32),
            shp((GROUP * SHARED, 256), BF16),
            shp((GROUP * SHARED, 256), BF16),
            shp((SHARED // 2, 384), BF16),
        ),
        [pltpu.VMEM((9, 14 * 16, CONV), BF16), pltpu.VMEM((CONV, OWN), F32)],
        specs=sm(1) + vm(6),
        us=3,
    )(info, *pieces, border, conv_weight)
    gother = swapped(gaway)
    gedge = exchanged(gedge, GROUP)
    *acts, gmix, gown, gsend = call(
        mixed_kernel,
        (
            *[shp((OWN, 128), BF16)] * GROUP,
            shp((OWN, WIDTH), F32),
            shp((OWN, WIDTH), BF16),
            shp((TAIL, WIDTH), BF16),
        ),
        specs=sm(1) + vm(5),
        us=1,
    )(info, own, branch, before, back, gout)
    gtail = passed_along(gsend, "win", -1)
    gtail, gedge, acts = lax.optimization_barrier((gtail, gedge, acts))
    acts = [acts[0]] + [exchanged(acts[d], d) for d in (1, 2, 3)]
    acts = jnp.concatenate(acts, 0)
    others = swapped(acts)
    eother = swapped(gedge)
    gqkv, keep, send = call(
        backward_kernel,
        (shp((ALL, 3 * WIDTH), BF16), shp((ALL, 1280), BF16), shp((ALL, 1280), BF16)),
        specs=sm(1) + vm(5),
        us=5,
    )(info, qkv, probs, gown, gtail, w_attn)
    other = swapped(send)
    total, gback = call(
        window_kernel,
        (shp((OWN, WIDTH), F32), shp((TAIL, WIDTH), BF16)),
        specs=vm(3),
        us=1,
    )(gqkv, w_attn, gmix)
    returned = passed_along(gback, "win", 1)
    anyspace = pl.BlockSpec(memory_space=pl.ANY)
    shares = call(
        conv_sum_kernel,
        shp((32, 8 * BLOCKS, 128), BF16),
        [
            pltpu.VMEM((ROWS_C + 16, 128), F32),
            pltpu.VMEM((SB + ROWS_C + 24, 128), F32),
            pltpu.VMEM((32, 8 * UNIT, 128), BF16),
            pltpu.SemaphoreType.DMA,
        ],
        specs=sm(1) + vm(6),
        out_specs=anyspace,
        us=4,
    )(info, acts, others, gkeep, gother, gedge, eother)
    shares = call(
        attn_sum_kernel,
        shp((32, 8 * BLOCKS, 128), BF16),
        [
            pltpu.VMEM((4 * WIDTH, 128), F32),
            pltpu.VMEM((4 * WIDTH, 128), F32),
            pltpu.VMEM((SB + 4 * WIDTH, 128), F32),
            pltpu.VMEM((32, 8 * (BLOCKS - UNIT), 128), BF16),
            pltpu.SemaphoreType.DMA,
        ],
        specs=vm(4) + [anyspace],
        out_specs=anyspace,
        aliases={4: 0},
        us=4,
    )(mine, theirs, keep, other, shares)
    devices = lax.axis_size("win") * lax.axis_size("tile")
    planes = [[32 * z + n for n in range(32)] for z in range(ROUND)]
    lines = [[32 * z + n for z in range(ROUND)] for n in range(32)]
    both = ("win", "tile")
    shares = lax.all_to_all(shares, both, 0, 0, tiled=True, axis_index_groups=planes)
    shares = call(
        gather_kernel,
        shp((ROUND, TOTALS + 6, 128), BF16),
        [pltpu.VMEM((8 * TOTALS + 48, 128), F32)],
        specs=vm(1),
        us=1.5,
    )(shares)
    shares = lax.all_to_all(shares, both, 0, 0, tiled=True, axis_index_groups=lines)

    factor = 1.0 / math.sqrt(STRIDE * 12 * devices)
    sums = jnp.sum(shares.astype(F32), axis=0) * factor
    conv = sums[: 8 * UNIT].reshape(2, GROUP, UNIT, 128)
    big = conv[:, :, :9].transpose(1, 2, 0, 3).reshape(GROUP, 9, 256)
    small = conv[:, :, 9:].reshape(2, GROUP, UNIT, 32)[:, :, :9]
    small = small.transpose(1, 2, 0, 3).reshape(GROUP, 9, 64)
    conv = jnp.concatenate([big, small], -1)
    begin = (2 * position + (135 * tile) // 4) % GROUP
    conv = lax.dynamic_slice(jnp.concatenate([conv, conv], 0), (begin, 0, 0), (GROUP, 9, CONV))
    conv = conv.transpose(1, 0, 2).reshape(-1)
    grad_conv = lax.dynamic_slice(conv, (240 * tile % 320,), (10800,))
    attn = sums[8 * UNIT : TOTALS].reshape(2, 5, 5, 128)
    big = attn[:, :, :4].reshape(2, 5, 2, 2, 128).transpose(2, 1, 0, 3, 4).reshape(10, 512)
    small = attn[:, :, 4].reshape(2, 5, 2, 64).transpose(2, 1, 0, 3).reshape(10, 128)
    grad_attn = jnp.concatenate([big, small], -1).reshape(-1)

    total = jnp.concatenate([total[:TAIL] + returned.astype(F32), total[TAIL:]], 0)
    grad_x = total.astype(BF16).reshape(STRIDE, 2, 8, WIDTH)[:, :, :6]
    return (grad_x, grad_attn, grad_conv)


def solution(mesh):
    placed = (P("win", "tile", None, None), P(), P(), P("win", None), P("win", "tile", None, None))
    return jax.shard_map(
        local,
        mesh=mesh,
        in_specs=placed,
        out_specs=(P("win", "tile", None, None), P(("win", "tile")), P(("win", "tile"))),
        check_vma=False,
    )
```

```python
import functools
import math

import jax
import jax.numpy as jnp
from jax import lax
from jax.experimental import pallas as pl
from jax.experimental.pallas import tpu as pltpu
from jax.sharding import PartitionSpec as P

HEADS = 10
CONV = 320
WIN_LEN = 16
STRIDE = 12
OVER = 4
WIDTH = 640
PLACES = 16
OWN = STRIDE * PLACES
TAIL = OVER * PLACES
ALL = OWN + TAIL
UNIT = 12
BLOCKS = 38
ROUND = 8
TOTALS = 8 * UNIT + 2 * 25
GROUP = 4
QUARTER = CONV // GROUP
SHARED = (STRIDE + 2) * 16
SB = 8
F32 = jnp.float32
BF16 = jnp.bfloat16
ROWS_C = 27 * QUARTER

NN = (((1,), (0,)), ((), ()))
NT = (((1,), (1,)), ((), ()))
TN = (((0,), (0,)), ((), ()))


def dot(a, b, dims=NN):
    return lax.dot_general(a, b, dims, preferred_element_type=F32)


def call(kernel, outs, scratch=(), specs=None, out_specs=None, aliases=None, us=1.0):
    if out_specs is None:
        out_specs = tuple(vm(len(outs))) if isinstance(outs, tuple) else vm(1)[0]
    return pl.pallas_call(
        kernel,
        out_shape=outs,
        in_specs=specs,
        out_specs=out_specs,
        scratch_shapes=scratch,
        input_output_aliases=aliases or {},
        compiler_params=pltpu.CompilerParams(vmem_limit_bytes=16 << 20),
        cost_estimate=pl.CostEstimate(
            flops=int(us * 1e9), bytes_accessed=int(us * 3e6), transcendentals=0
        ),
    )


def vm(n):
    return [pl.BlockSpec(memory_space=pltpu.VMEM)] * n


def sm(n):
    return [pl.BlockSpec(memory_space=pltpu.SMEM)] * n


def shp(shape, dtype):
    return jax.ShapeDtypeStruct(shape, dtype)


def lane_half(rows):
    return lax.broadcasted_iota(jnp.int32, (rows, 128), 1) < 64


def forward_kernel(info, fade, own, tail, w, qkv, probs, mine, branch, carried):
    x = jnp.concatenate([own[...], tail[:TAIL]], 0)
    mine[:, :WIDTH] = x
    for k in range(3):
        qkv[:, WIDTH * k : WIDTH * (k + 1)] = dot(x, w[k]).astype(BF16)
    scale = 64 ** (-0.5)
    row = lax.broadcasted_iota(jnp.int32, (ALL, ALL), 0)
    col = lax.broadcasted_iota(jnp.int32, (ALL, ALL), 1)
    limit = ALL - TAIL * info[0]
    bias = jnp.where((((row ^ col) & (PLACES - 1)) == 0) & (col < limit), 0.0, -1e30)
    first = lane_half(ALL)
    for pair in range(HEADS // 2):
        at = 128 * pair
        q = qkv[:, at : at + 128]
        k = qkv[:, WIDTH + at : WIDTH + at + 128]
        v = qkv[:, 2 * WIDTH + at : 2 * WIDTH + at + 128]
        results = []
        for side in range(2):
            picked = jnp.where(first if side == 0 else ~first, q, jnp.zeros_like(q))
            scores = dot(picked, k, NT) * scale + bias
            expo = jnp.exp(scores - jnp.max(scores, axis=-1, keepdims=True))
            prob = expo * (1.0 / jnp.sum(expo, axis=-1, keepdims=True))
            probs[2 * pair + side] = prob
            results.append(dot(prob.astype(BF16), v))
        mine[:, WIDTH + at : WIDTH + at + 128] = jnp.where(first, results[0], results[1]).astype(BF16)
    out = dot(mine[:, WIDTH:], w[3])
    branch[...] = out[:OWN]
    lines = lax.broadcasted_iota(jnp.int32, (16, WIDTH), 0)
    table = jnp.zeros((16, WIDTH), F32)
    for t in range(OVER):
        frac = fade[0, t].astype(F32) / 16.0
        part = out[OWN + PLACES * t : OWN + PLACES * (t + 1)]
        carried[PLACES * t : PLACES * (t + 1)] = (frac * part).astype(BF16)
        table = jnp.where(lines == t, frac, table)
    carried[TAIL:] = table.astype(BF16)


def shifted(g, c):
    if c == 1:
        return jnp.concatenate([g[-1:], g[:-1]], 0)
    if c == -1:
        return jnp.concatenate([g[1:], g[:1]], 0)
    return g


def slab_of(g, b, c, frames, rows):
    width = g.shape[-1]
    lines = shifted(g, c).reshape(frames, 8 * (rows + 2), width)
    lines = lines[:, 8 * (1 - b) : 8 * (1 - b) + 8 * rows, :]
    return lines.astype(BF16).reshape(frames * 8 * rows, width)


def conv_back_kernel(info, g0, g1, g2, g3, edge, w, out, keep, send, away, slabs, acc):
    x, upper = info[2], info[3]
    lower = info[1] == 0
    row = (x ^ (GROUP - 1)) * (1 - upper) + x * upper
    border = jnp.zeros((SHARED, 384), BF16)
    for d, g in enumerate((g0, g1, g2, g3)):
        at = slice(SHARED * d, SHARED * (d + 1))
        left, right, end = g[:, :128], g[:, 128:256], g[:, 256:]
        keep[at, :128] = jnp.where(lower, left, right)
        send[at, :128] = jnp.where(lower, right, left)
        keep[at, 128:] = end
        send[at, 128:] = end
        border = jnp.where(row == d, g[...], border)
    border = border.astype(F32).reshape(STRIDE + 2, 16, 384)
    border = jnp.where(upper == 0, border[:, 8:], border[:, :8])
    away[...] = border.reshape(SHARED // 2, 384).astype(BF16)
    border = edge[...].astype(F32).reshape(STRIDE + 2, 8, 384)
    parts = [g[...].astype(F32).reshape(STRIDE + 2, 16, 384) for g in (g0, g1, g2, g3)]

    def row_of(n, half):
        return parts[n][:, 8 * half : 8 * half + 8]

    blank = jnp.zeros_like(border)
    low = jnp.where(x == 0, jnp.where(upper == 1, border, blank), row_of(1, 1))
    low = jnp.where(x == 2, row_of(3, 1), low)
    high = jnp.where(x == 3, jnp.where(upper == 1, blank, border), row_of(1, 0))
    high = jnp.where(x == 1, row_of(3, 0), high)
    lines = jnp.concatenate([low, parts[0], high], 1).reshape((STRIDE + 2) * 32, 384)
    lines = lines[:, :CONV]
    for b in (-1, 0, 1):
        for c in (-1, 0, 1):
            slabs[3 * (b + 1) + c + 1] = slab_of(lines, b, c, STRIDE + 2, 2)
    for a in (-1, 0, 1):
        for j in range(9):
            part = slabs[j, 16 * (1 - a) : 16 * (1 - a) + OWN, :]
            term = dot(w[9 * (a + 1) + j], part, NT)
            if a == -1 and j == 0:
                acc[...] = term
            else:
                acc[...] += term
    out[...] = acc[...].T


def mixed_kernel(
    info, own, branch, before, back, gout, act0, act1, act2, act3, gmix, gown, gsend
):
    lines = lax.broadcasted_iota(jnp.int32, (OWN, 1), 0)
    inside = (lines & 7) < 6
    prev = jnp.zeros((TAIL, 1), F32)
    for t in range(OVER):
        value = before[TAIL + t : TAIL + t + 1, 0:1].astype(F32)
        prev = jnp.where((lines[:TAIL] >> 4) == t, value, prev)
    head = 1.0 - prev
    top = head * branch[:TAIL] + before[:TAIL].astype(F32)
    mixed = own[...].astype(F32) + jnp.concatenate([top, branch[TAIL:]], 0)
    conv_in = mixed[:, :CONV]
    sig = 1.0 / (1.0 + jnp.exp(-conv_in))
    value = (conv_in * sig).astype(BF16)
    channel = lax.broadcasted_iota(jnp.int32, (CONV, 128), 0)
    column = lax.broadcasted_iota(jnp.int32, (CONV, 128), 1)
    for d in range(GROUP):
        wanted = GROUP * column + (info[2] ^ d)
        pick = jnp.where((channel == wanted) & (column < QUARTER), 1.0, 0.0).astype(BF16)
        (act0, act1, act2, act3)[d][...] = dot(value, pick).astype(BF16)
    slope = sig * (1.0 + conv_in * (1.0 - sig))
    extra = jnp.where(inside, back[...] * slope, 0.0)
    gmix[...] = gout[...].astype(F32)
    gmix[:, :CONV] += extra
    total = gmix[...]
    beta = jnp.concatenate([head, jnp.ones((OWN - TAIL, 1), F32)], 0)
    gown[...] = (beta * total).astype(BF16)
    gsend[...] = (prev * total[:TAIL]).astype(BF16)


def backward_kernel(info, qkv, probs, gown, gtail, w, gqkv, keep, send):
    scale = 64 ** (-0.5)
    gb = jnp.concatenate([gown[...], gtail[...]], 0)
    gh = dot(gb, w[3], NT).astype(BF16)
    first = lane_half(ALL)
    zero = jnp.zeros((ALL, 128), BF16)
    for pair in range(HEADS // 2):
        at = 128 * pair
        q = qkv[:, at : at + 128]
        k = qkv[:, WIDTH + at : WIDTH + at + 128]
        v = qkv[:, 2 * WIDTH + at : 2 * WIDTH + at + 128]
        g = gh[:, at : at + 128]
        results = []
        for side in range(2):
            prob = probs[2 * pair + side]
            gp = dot(jnp.where(first if side == 0 else ~first, g, zero), v, NT)
            inner = jnp.sum(prob * gp, axis=-1, keepdims=True)
            gs = (prob * (gp - inner) * scale).astype(BF16)
            results.append((dot(gs, k), dot(gs, q, TN), dot(prob.astype(BF16), g, TN)))
        for n in range(3):
            picked = jnp.where(first, results[0][n], results[1][n])
            gqkv[:, WIDTH * n + at : WIDTH * n + at + 128] = picked.astype(BF16)
    lower = info[1] == 0
    ends = []
    for n in range(4):
        part = gqkv[:, WIDTH * n : WIDTH * (n + 1)] if n < 3 else gb
        low, high = part[:, :256], part[:, 256:512]
        keep[:, 256 * n : 256 * (n + 1)] = jnp.where(lower, low, high)
        send[:, 256 * n : 256 * (n + 1)] = jnp.where(lower, high, low)
        ends.append(part[:, 512:])
    for n in range(2):
        one, two = ends[2 * n], ends[2 * n + 1]
        low = jnp.concatenate([one[:, :64], two[:, :64]], 1)
        high = jnp.concatenate([one[:, 64:], two[:, 64:]], 1)
        keep[:, 1024 + 128 * n : 1152 + 128 * n] = jnp.where(lower, low, high)
        send[:, 1024 + 128 * n : 1152 + 128 * n] = jnp.where(lower, high, low)


def window_kernel(gqkv, w, gmix, total, back):
    acc = dot(gqkv[:, :WIDTH], w[0], NT)
    acc += dot(gqkv[:, WIDTH : 2 * WIDTH], w[1], NT)
    acc += dot(gqkv[:, 2 * WIDTH :], w[2], NT)
    total[...] = gmix[...] + acc[:OWN]
    back[...] = acc[OWN:].astype(BF16)


def conv_sum_kernel(info, a1, a2, g1, g2, e1, e2, out, wide, narrow, stage, sem):
    x, upper = info[2], info[3]
    frames = STRIDE + 2
    half = CONV // 2
    left = [[], [], []]
    lines = []
    gap = jnp.zeros((QUARTER, 64), BF16)
    for act, g, e in ((a1, g1, e1), (a2, g2, e2)):
        places = [pl.ds(pl.multiple_of(OWN * (x ^ n), 16), OWN) for n in range(GROUP)]
        rows = [act[at, :].reshape(STRIDE, 1, 16, 128) for at in places]
        turned = jnp.concatenate(rows, 1).reshape(STRIDE * 64, 128).T[:QUARTER]
        left[0] += [gap, gap, turned]
        left[1] += [gap, turned, gap]
        left[2] += [turned, gap, gap]

        def cut(value):
            value = value.astype(F32)
            end = value[:, 128:]
            end = jnp.where(info[1] == 0, end, pltpu.roll(end, 96, 1))[:, :32]
            return jnp.concatenate([value[:, :128], end], 1).reshape(frames, -1, half)

        border = e[...]
        start = jnp.where(info[1] == 0, border[:, :128], border[:, 128:256])
        border = cut(jnp.concatenate([start, border[:, 256:]], 1))
        before = jnp.where(upper == 1, border, 0.0)
        after = jnp.where(upper == 1, 0.0, border)
        places = [pl.ds(pl.multiple_of(SHARED * (x ^ n), 16), SHARED) for n in range(GROUP)]
        inner = [cut(g[at, :]) for at in places]
        lines.append(jnp.concatenate([before] + inner + [after], 1).reshape(frames * 80, half))
    left = jnp.concatenate([jnp.concatenate(line, 1) for line in left], 0)
    wide[ROWS_C:, :] = jnp.zeros((16, 128), F32)
    narrow[...] = jnp.zeros(narrow.shape, F32)
    for b in (-1, 0, 1):
        for c in (-1, 0, 1):
            slabs = [slab_of(line, b, c, frames, 8) for line in lines]
            part = dot(left, jnp.concatenate(slabs, 0))
            for a in range(3):
                at = QUARTER * (9 * a + 3 * (b + 1) + c + 1)
                block = part[QUARTER * a : QUARTER * (a + 1)]
                wide[at : at + QUARTER, :] = block[:, :128]
                for q in range(4):
                    start = SB + at - q
                    narrow[start : start + QUARTER, 32 * q : 32 * (q + 1)] = block[:, 128:]
    for t in range(8):
        for p in range(2):
            start = (270 * p + (135 * t) // 4 - x + 3) >> 2
            for y in range(2):
                blocks = []
                for n in range(UNIT):
                    if n < 9:
                        rows = pl.ds(start + 135 * y + n, ROUND, stride=270)
                        blocks.append(wide[rows, :])
                    else:
                        rows = pl.ds(SB + start + 135 * y + 4 * (n - 9), ROUND, stride=270)
                        blocks.append(narrow[rows, :])
                share = 8 * (2 * y + p) + t
                for n in range(0, UNIT, 2):
                    pair = jnp.concatenate(blocks[n : n + 2], 0).astype(BF16)
                    stage[share, 8 * n : 8 * n + 16] = pair
    copy = pltpu.make_async_copy(stage, out.at[:, 0 : 8 * UNIT], sem)
    copy.start()
    copy.wait()


def attn_sum_kernel(a1, a2, b1, b2, held, out, low, high, ends, stage, sem):
    del held
    turned = jnp.concatenate([a1[...], a2[...]], 0).T
    b = jnp.concatenate([b1[...], b2[...]], 0)
    flat, heads = turned[:WIDTH], turned[WIDTH:]
    part = dot(flat, b[:, : 3 * 256])
    for k in range(3):
        low[WIDTH * k : WIDTH * (k + 1), :] = part[:, 256 * k : 256 * k + 128]
        high[WIDTH * k : WIDTH * (k + 1), :] = part[:, 256 * k + 128 : 256 * (k + 1)]
    part = dot(heads, b[:, 3 * 256 : 4 * 256])
    low[3 * WIDTH :, :] = part[:, :128]
    high[3 * WIDTH :, :] = part[:, 128:]
    tail = b[:, 1152:]
    first = lane_half(WIDTH)
    pairs = (dot(flat, b[:, 1024:1152]), jnp.where(first, dot(flat, tail), dot(heads, tail)))
    for k in range(4):
        plain = pairs[k // 2]
        rolled = pltpu.roll(plain, 64, 1)
        here, there = (plain, rolled) if k % 2 == 0 else (rolled, plain)
        ends[SB + WIDTH * k : SB + WIDTH * (k + 1), :64] = here[:, :64]
        at = SB + WIDTH * k - 5
        ends[at : at + WIDTH, 64:] = there[:, 64:]
    for share in range(32):
        blocks = []
        for e in range(5):
            one = 80 * (share // 8) + 10 * (share % 8) + e
            rows = pl.ds(one, ROUND, stride=320)
            more = pl.ds(one + 5, ROUND, stride=320)
            blocks += [low[rows, :], high[rows, :], low[more, :], high[more, :]]
            blocks.append(ends[pl.ds(SB + one, ROUND, stride=320), :])
        blocks.append(jnp.zeros((ROUND, 128), F32))
        for n in range(0, 26, 2):
            pair = jnp.concatenate(blocks[n : n + 2], 0).astype(BF16)
            stage[share, 8 * n : 8 * n + 16] = pair
    copy = pltpu.make_async_copy(stage, out.at[:, 8 * UNIT :], sem)
    copy.start()
    copy.wait()


def gather_kernel(given, out, sums):
    def added(sources, rows):
        total = given[sources[0], rows].astype(F32)
        for n in sources[1:]:
            total += given[n, rows].astype(F32)
        return total

    count = 8 * UNIT
    for c in range(2):
        for n in range(GROUP):
            sources = [8 * (2 * y + c) + GROUP * h + n for y in range(2) for h in range(2)]
            at = count * (GROUP * c + n)
            sums[at : at + count, :] = added(sources, slice(0, count))
        sources = [8 * (2 * y + c) + t for y in range(2) for t in range(8)]
        at = 8 * (count + 25 * c)
        sums[at : at + 200, :] = added(sources, slice(count, count + 208))[:200]
    sums[8 * TOTALS :, :] = jnp.zeros((48, 128), F32)
    for z in range(ROUND):
        out[z] = sums[pl.ds(z, TOTALS + 6, stride=8), :].astype(BF16)


def passed_along(block, axis, distance):
    devices = range(lax.axis_size(axis))
    route = [(i - distance, i) for i in devices if i - distance in devices]
    return lax.ppermute(block, axis, route)


def swapped(block):
    return lax.ppermute(block, "win", [(i, i ^ 1) for i in range(lax.axis_size("win"))])


def exchanged(block, distance):
    return lax.ppermute(block, "tile", [(i, i ^ distance) for i in range(lax.axis_size("tile"))])


def local(frames_in, w_attn, conv_weight, fade, grad_out):
    position = lax.axis_index("win")
    tile = lax.axis_index("tile")
    core = position % 2
    last = position == lax.axis_size("win") - 1
    info = jnp.stack([last, core, tile % GROUP, tile // GROUP]).astype(jnp.int32)
    pad = ((0, 0), (0, 0), (0, 2), (0, 0))
    own = jnp.pad(frames_in, pad).reshape(OWN, WIDTH)
    gpad = jnp.pad(grad_out, pad)
    gout = gpad.reshape(OWN, WIDTH)
    gframes = jnp.pad(gpad[..., :CONV], ((0, 0), (0, 0), (0, 0), (0, 64)))
    gframes = gframes.reshape(OWN, 384)
    first = jnp.pad(gpad[0, ..., :CONV].reshape(16, CONV), ((0, 0), (0, CONV)))
    tail = passed_along(jnp.concatenate([own[:TAIL], first], 0), "win", -1)
    before = passed_along(gframes[OWN - 16 :], "win", 1)
    gframes = jnp.concatenate([before, gframes, tail[TAIL:, :384]], 0)
    pieces = [gframes] + [exchanged(gframes, d) for d in (1, 2, 3)]
    sides = gframes.reshape(STRIDE + 2, 2, 8, 384)
    sides = jnp.where(tile < GROUP, sides[:, 1], sides[:, 0]).reshape(SHARED // 2, 384)
    border = lax.ppermute(sides, "tile", [(GROUP - 1, GROUP), (GROUP, GROUP - 1)])

    qkv, probs, mine, branch, carried = call(
        forward_kernel,
        (
            shp((ALL, 3 * WIDTH), BF16),
            shp((HEADS, ALL, ALL), F32),
            shp((ALL, 2 * WIDTH), BF16),
            shp((OWN, WIDTH), F32),
            shp((TAIL + 16, WIDTH), BF16),
        ),
        specs=sm(2) + vm(3),
        us=4,
    )(info, fade, own, tail, w_attn)
    before = passed_along(carried, "win", 1)
    theirs = swapped(mine)
    back, gkeep, gaway, gedge = call(
        conv_back_kernel,
        (
            shp((OWN, CONV), F32),
            shp((GROUP * SHARED, 256), BF16),
            shp((GROUP * SHARED, 256), BF16),
            shp((SHARED // 2, 384), BF16),
        ),
        [pltpu.VMEM((9, 14 * 16, CONV), BF16), pltpu.VMEM((CONV, OWN), F32)],
        specs=sm(1) + vm(6),
        us=3,
    )(info, *pieces, border, conv_weight)
    gother = swapped(gaway)
    *acts, gmix, gown, gsend = call(
        mixed_kernel,
        (
            *[shp((OWN, 128), BF16)] * GROUP,
            shp((OWN, WIDTH), F32),
            shp((OWN, WIDTH), BF16),
            shp((TAIL, WIDTH), BF16),
        ),
        specs=sm(1) + vm(5),
        us=1,
    )(info, own, branch, before, back, gout)
    gedge, gown = lax.optimization_barrier((gedge, gown))
    gedge = exchanged(gedge, GROUP)
    gtail = passed_along(gsend, "win", -1)
    gtail, gedge, acts = lax.optimization_barrier((gtail, gedge, acts))
    acts = [acts[0]] + [exchanged(acts[d], d) for d in (1, 2, 3)]
    acts = jnp.concatenate(acts, 0)
    others = swapped(acts)
    eother = swapped(gedge)
    gqkv, keep, send = call(
        backward_kernel,
        (shp((ALL, 3 * WIDTH), BF16), shp((ALL, 1280), BF16), shp((ALL, 1280), BF16)),
        specs=sm(1) + vm(5),
        us=5,
    )(info, qkv, probs, gown, gtail, w_attn)
    other = swapped(send)
    total, gback = call(
        window_kernel,
        (shp((OWN, WIDTH), F32), shp((TAIL, WIDTH), BF16)),
        specs=vm(3),
        us=1,
    )(gqkv, w_attn, gmix)
    returned = passed_along(gback, "win", 1)
    anyspace = pl.BlockSpec(memory_space=pl.ANY)
    shares = call(
        conv_sum_kernel,
        shp((32, 8 * BLOCKS, 128), BF16),
        [
            pltpu.VMEM((ROWS_C + 16, 128), F32),
            pltpu.VMEM((SB + ROWS_C + 24, 128), F32),
            pltpu.VMEM((32, 8 * UNIT, 128), BF16),
            pltpu.SemaphoreType.DMA,
        ],
        specs=sm(1) + vm(6),
        out_specs=anyspace,
        us=4,
    )(info, acts, others, gkeep, gother, gedge, eother)
    shares = call(
        attn_sum_kernel,
        shp((32, 8 * BLOCKS, 128), BF16),
        [
            pltpu.VMEM((4 * WIDTH, 128), F32),
            pltpu.VMEM((4 * WIDTH, 128), F32),
            pltpu.VMEM((SB + 4 * WIDTH, 128), F32),
            pltpu.VMEM((32, 8 * (BLOCKS - UNIT), 128), BF16),
            pltpu.SemaphoreType.DMA,
        ],
        specs=vm(4) + [anyspace],
        out_specs=anyspace,
        aliases={4: 0},
        us=4,
    )(mine, theirs, keep, other, shares)
    devices = lax.axis_size("win") * lax.axis_size("tile")
    planes = [[32 * z + n for n in range(32)] for z in range(ROUND)]
    lines = [[32 * z + n for z in range(ROUND)] for n in range(32)]
    both = ("win", "tile")
    shares = lax.all_to_all(shares, both, 0, 0, tiled=True, axis_index_groups=planes)
    shares = call(
        gather_kernel,
        shp((ROUND, TOTALS + 6, 128), BF16),
        [pltpu.VMEM((8 * TOTALS + 48, 128), F32)],
        specs=vm(1),
        us=1.5,
    )(shares)
    shares = lax.all_to_all(shares, both, 0, 0, tiled=True, axis_index_groups=lines)

    factor = 1.0 / math.sqrt(STRIDE * 12 * devices)
    sums = jnp.sum(shares.astype(F32), axis=0) * factor
    conv = sums[: 8 * UNIT].reshape(2, GROUP, UNIT, 128)
    big = conv[:, :, :9].transpose(1, 2, 0, 3).reshape(GROUP, 9, 256)
    small = conv[:, :, 9:].reshape(2, GROUP, UNIT, 32)[:, :, :9]
    small = small.transpose(1, 2, 0, 3).reshape(GROUP, 9, 64)
    conv = jnp.concatenate([big, small], -1)
    begin = (2 * position + (135 * tile) // 4) % GROUP
    conv = lax.dynamic_slice(jnp.concatenate([conv, conv], 0), (begin, 0, 0), (GROUP, 9, CONV))
    conv = conv.transpose(1, 0, 2).reshape(-1)
    grad_conv = lax.dynamic_slice(conv, (240 * tile % 320,), (10800,))
    attn = sums[8 * UNIT : TOTALS].reshape(2, 5, 5, 128)
    big = attn[:, :, :4].reshape(2, 5, 2, 2, 128).transpose(2, 1, 0, 3, 4).reshape(10, 512)
    small = attn[:, :, 4].reshape(2, 5, 2, 64).transpose(2, 1, 0, 3).reshape(10, 128)
    grad_attn = jnp.concatenate([big, small], -1).reshape(-1)

    total = jnp.concatenate([total[:TAIL] + returned.astype(F32), total[TAIL:]], 0)
    grad_x = total.astype(BF16).reshape(STRIDE, 2, 8, WIDTH)[:, :, :6]
    return (grad_x, grad_attn, grad_conv)


def solution(mesh):
    placed = (P("win", "tile", None, None), P(), P(), P("win", None), P("win", "tile", None, None))
    return jax.shard_map(
        local,
        mesh=mesh,
        in_specs=placed,
        out_specs=(P("win", "tile", None, None), P(("win", "tile")), P(("win", "tile"))),
        check_vma=False,
    )
```

```python
import functools
import math

import jax
import jax.numpy as jnp
from jax import lax
from jax.experimental import pallas as pl
from jax.experimental.pallas import tpu as pltpu
from jax.sharding import PartitionSpec as P

HEADS = 10
CONV = 320
WIN_LEN = 16
STRIDE = 12
OVER = 4
WIDTH = 640
PLACES = 16
OWN = STRIDE * PLACES
TAIL = OVER * PLACES
ALL = OWN + TAIL
UNIT = 12
BLOCKS = 38
ROUND = 8
TOTALS = 8 * UNIT + 2 * 25
GROUP = 4
QUARTER = CONV // GROUP
SHARED = (STRIDE + 2) * 16
SB = 8
F32 = jnp.float32
BF16 = jnp.bfloat16
ROWS_C = 27 * QUARTER

NN = (((1,), (0,)), ((), ()))
NT = (((1,), (1,)), ((), ()))
TN = (((0,), (0,)), ((), ()))


def dot(a, b, dims=NN):
    return lax.dot_general(a, b, dims, preferred_element_type=F32)


def call(kernel, outs, scratch=(), specs=None, out_specs=None, aliases=None, us=1.0):
    if out_specs is None:
        out_specs = tuple(vm(len(outs))) if isinstance(outs, tuple) else vm(1)[0]
    return pl.pallas_call(
        kernel,
        out_shape=outs,
        in_specs=specs,
        out_specs=out_specs,
        scratch_shapes=scratch,
        input_output_aliases=aliases or {},
        compiler_params=pltpu.CompilerParams(vmem_limit_bytes=16 << 20),
        cost_estimate=pl.CostEstimate(
            flops=int(us * 1e9), bytes_accessed=int(us * 3e6), transcendentals=0
        ),
    )


def vm(n):
    return [pl.BlockSpec(memory_space=pltpu.VMEM)] * n


def sm(n):
    return [pl.BlockSpec(memory_space=pltpu.SMEM)] * n


def shp(shape, dtype):
    return jax.ShapeDtypeStruct(shape, dtype)


def lane_half(rows):
    return lax.broadcasted_iota(jnp.int32, (rows, 128), 1) < 64


def forward_kernel(info, fade, own, tail, w, qkv, probs, mine, branch, carried):
    x = jnp.concatenate([own[...], tail[:TAIL]], 0)
    mine[:, :WIDTH] = x
    for k in range(3):
        qkv[:, WIDTH * k : WIDTH * (k + 1)] = dot(x, w[k]).astype(BF16)
    scale = 64 ** (-0.5)
    row = lax.broadcasted_iota(jnp.int32, (ALL, ALL), 0)
    col = lax.broadcasted_iota(jnp.int32, (ALL, ALL), 1)
    limit = ALL - TAIL * info[0]
    bias = jnp.where((((row ^ col) & (PLACES - 1)) == 0) & (col < limit), 0.0, -1e30)
    first = lane_half(ALL)
    for pair in range(HEADS // 2):
        at = 128 * pair
        q = qkv[:, at : at + 128]
        k = qkv[:, WIDTH + at : WIDTH + at + 128]
        v = qkv[:, 2 * WIDTH + at : 2 * WIDTH + at + 128]
        results = []
        for side in range(2):
            picked = jnp.where(first if side == 0 else ~first, q, jnp.zeros_like(q))
            scores = dot(picked, k, NT) * scale + bias
            expo = jnp.exp(scores - jnp.max(scores, axis=-1, keepdims=True))
            prob = expo * (1.0 / jnp.sum(expo, axis=-1, keepdims=True))
            probs[2 * pair + side] = prob
            results.append(dot(prob.astype(BF16), v))
        mine[:, WIDTH + at : WIDTH + at + 128] = jnp.where(first, results[0], results[1]).astype(BF16)
    out = dot(mine[:, WIDTH:], w[3])
    branch[...] = out[:OWN]
    lines = lax.broadcasted_iota(jnp.int32, (16, WIDTH), 0)
    table = jnp.zeros((16, WIDTH), F32)
    for t in range(OVER):
        frac = fade[0, t].astype(F32) / 16.0
        part = out[OWN + PLACES * t : OWN + PLACES * (t + 1)]
        carried[PLACES * t : PLACES * (t + 1)] = (frac * part).astype(BF16)
        table = jnp.where(lines == t, frac, table)
    carried[TAIL:] = table.astype(BF16)


def shifted(g, c):
    if c == 1:
        return jnp.concatenate([g[-1:], g[:-1]], 0)
    if c == -1:
        return jnp.concatenate([g[1:], g[:1]], 0)
    return g


def slab_of(g, b, c, frames, rows):
    width = g.shape[-1]
    lines = shifted(g, c).reshape(frames, 8 * (rows + 2), width)
    lines = lines[:, 8 * (1 - b) : 8 * (1 - b) + 8 * rows, :]
    return lines.astype(BF16).reshape(frames * 8 * rows, width)


def conv_back_kernel(info, g0, g1, g2, g3, edge, w, out, keep, send, away, slabs, acc):
    x, upper = info[2], info[3]
    lower = info[1] == 0
    row = (x ^ (GROUP - 1)) * (1 - upper) + x * upper
    border = jnp.zeros((SHARED, 384), BF16)
    for d, g in enumerate((g0, g1, g2, g3)):
        at = slice(SHARED * d, SHARED * (d + 1))
        left, right, end = g[:, :128], g[:, 128:256], g[:, 256:]
        keep[at, :128] = jnp.where(lower, left, right)
        send[at, :128] = jnp.where(lower, right, left)
        keep[at, 128:] = end
        send[at, 128:] = end
        border = jnp.where(row == d, g[...], border)
    border = border.astype(F32).reshape(STRIDE + 2, 16, 384)
    border = jnp.where(upper == 0, border[:, 8:], border[:, :8])
    away[...] = border.reshape(SHARED // 2, 384).astype(BF16)
    border = edge[...].astype(F32).reshape(STRIDE + 2, 8, 384)
    parts = [g[...].astype(F32).reshape(STRIDE + 2, 16, 384) for g in (g0, g1, g2, g3)]

    def row_of(n, half):
        return parts[n][:, 8 * half : 8 * half + 8]

    blank = jnp.zeros_like(border)
    low = jnp.where(x == 0, jnp.where(upper == 1, border, blank), row_of(1, 1))
    low = jnp.where(x == 2, row_of(3, 1), low)
    high = jnp.where(x == 3, jnp.where(upper == 1, blank, border), row_of(1, 0))
    high = jnp.where(x == 1, row_of(3, 0), high)
    lines = jnp.concatenate([low, parts[0], high], 1).reshape((STRIDE + 2) * 32, 384)
    lines = lines[:, :CONV]
    for b in (-1, 0, 1):
        for c in (-1, 0, 1):
            slabs[3 * (b + 1) + c + 1] = slab_of(lines, b, c, STRIDE + 2, 2)
    for a in (-1, 0, 1):
        for j in range(9):
            part = slabs[j, 16 * (1 - a) : 16 * (1 - a) + OWN, :]
            term = dot(w[9 * (a + 1) + j], part, NT)
            if a == -1 and j == 0:
                acc[...] = term
            else:
                acc[...] += term
    out[...] = acc[...].T


def mixed_kernel(
    info, own, branch, before, back, gout, act0, act1, act2, act3, gmix, gown, gsend
):
    lines = lax.broadcasted_iota(jnp.int32, (OWN, 1), 0)
    inside = (lines & 7) < 6
    prev = jnp.zeros((TAIL, 1), F32)
    for t in range(OVER):
        value = before[TAIL + t : TAIL + t + 1, 0:1].astype(F32)
        prev = jnp.where((lines[:TAIL] >> 4) == t, value, prev)
    head = 1.0 - prev
    top = head * branch[:TAIL] + before[:TAIL].astype(F32)
    mixed = own[...].astype(F32) + jnp.concatenate([top, branch[TAIL:]], 0)
    conv_in = mixed[:, :CONV]
    sig = 1.0 / (1.0 + jnp.exp(-conv_in))
    value = (conv_in * sig).astype(BF16)
    channel = lax.broadcasted_iota(jnp.int32, (CONV, 128), 0)
    column = lax.broadcasted_iota(jnp.int32, (CONV, 128), 1)
    for d in range(GROUP):
        wanted = GROUP * column + (info[2] ^ d)
        pick = jnp.where((channel == wanted) & (column < QUARTER), 1.0, 0.0).astype(BF16)
        (act0, act1, act2, act3)[d][...] = dot(value, pick).astype(BF16)
    slope = sig * (1.0 + conv_in * (1.0 - sig))
    extra = jnp.where(inside, back[...] * slope, 0.0)
    gmix[...] = gout[...].astype(F32)
    gmix[:, :CONV] += extra
    total = gmix[...]
    beta = jnp.concatenate([head, jnp.ones((OWN - TAIL, 1), F32)], 0)
    gown[...] = (beta * total).astype(BF16)
    gsend[...] = (prev * total[:TAIL]).astype(BF16)


def backward_kernel(info, qkv, probs, gown, gtail, w, gqkv, keep, send):
    scale = 64 ** (-0.5)
    gb = jnp.concatenate([gown[...], gtail[...]], 0)
    gh = dot(gb, w[3], NT).astype(BF16)
    first = lane_half(ALL)
    zero = jnp.zeros((ALL, 128), BF16)
    for pair in range(HEADS // 2):
        at = 128 * pair
        q = qkv[:, at : at + 128]
        k = qkv[:, WIDTH + at : WIDTH + at + 128]
        v = qkv[:, 2 * WIDTH + at : 2 * WIDTH + at + 128]
        g = gh[:, at : at + 128]
        results = []
        for side in range(2):
            prob = probs[2 * pair + side]
            gp = dot(jnp.where(first if side == 0 else ~first, g, zero), v, NT)
            inner = jnp.sum(prob * gp, axis=-1, keepdims=True)
            gs = (prob * (gp - inner) * scale).astype(BF16)
            results.append((dot(gs, k), dot(gs, q, TN), dot(prob.astype(BF16), g, TN)))
        for n in range(3):
            picked = jnp.where(first, results[0][n], results[1][n])
            gqkv[:, WIDTH * n + at : WIDTH * n + at + 128] = picked.astype(BF16)
    lower = info[1] == 0
    ends = []
    for n in range(4):
        part = gqkv[:, WIDTH * n : WIDTH * (n + 1)] if n < 3 else gb
        low, high = part[:, :256], part[:, 256:512]
        keep[:, 256 * n : 256 * (n + 1)] = jnp.where(lower, low, high)
        send[:, 256 * n : 256 * (n + 1)] = jnp.where(lower, high, low)
        ends.append(part[:, 512:])
    for n in range(2):
        one, two = ends[2 * n], ends[2 * n + 1]
        low = jnp.concatenate([one[:, :64], two[:, :64]], 1)
        high = jnp.concatenate([one[:, 64:], two[:, 64:]], 1)
        keep[:, 1024 + 128 * n : 1152 + 128 * n] = jnp.where(lower, low, high)
        send[:, 1024 + 128 * n : 1152 + 128 * n] = jnp.where(lower, high, low)


def window_kernel(gqkv, w, gmix, total, back):
    acc = dot(gqkv[:, :WIDTH], w[0], NT)
    acc += dot(gqkv[:, WIDTH : 2 * WIDTH], w[1], NT)
    acc += dot(gqkv[:, 2 * WIDTH :], w[2], NT)
    total[...] = gmix[...] + acc[:OWN]
    back[...] = acc[OWN:].astype(BF16)


def conv_sum_kernel(info, a1, a2, g1, g2, e1, e2, out, wide, narrow):
    x, upper = info[2], info[3]
    frames = STRIDE + 2
    half = CONV // 2
    left = [[], [], []]
    lines = []
    gap = jnp.zeros((QUARTER, 64), BF16)
    for act, g, e in ((a1, g1, e1), (a2, g2, e2)):
        places = [pl.ds(pl.multiple_of(OWN * (x ^ n), 16), OWN) for n in range(GROUP)]
        rows = [act[at, :].reshape(STRIDE, 1, 16, 128) for at in places]
        turned = jnp.concatenate(rows, 1).reshape(STRIDE * 64, 128).T[:QUARTER]
        left[0] += [gap, gap, turned]
        left[1] += [gap, turned, gap]
        left[2] += [turned, gap, gap]

        def cut(value):
            value = value.astype(F32)
            end = value[:, 128:]
            end = jnp.where(info[1] == 0, end, pltpu.roll(end, 96, 1))[:, :32]
            return jnp.concatenate([value[:, :128], end], 1).reshape(frames, -1, half)

        border = e[...]
        start = jnp.where(info[1] == 0, border[:, :128], border[:, 128:256])
        border = cut(jnp.concatenate([start, border[:, 256:]], 1))
        before = jnp.where(upper == 1, border, 0.0)
        after = jnp.where(upper == 1, 0.0, border)
        places = [pl.ds(pl.multiple_of(SHARED * (x ^ n), 16), SHARED) for n in range(GROUP)]
        inner = [cut(g[at, :]) for at in places]
        lines.append(jnp.concatenate([before] + inner + [after], 1).reshape(frames * 80, half))
    left = jnp.concatenate([jnp.concatenate(line, 1) for line in left], 0)
    wide[ROWS_C:, :] = jnp.zeros((16, 128), F32)
    narrow[...] = jnp.zeros(narrow.shape, F32)
    for b in (-1, 0, 1):
        for c in (-1, 0, 1):
            slabs = [slab_of(line, b, c, frames, 8) for line in lines]
            part = dot(left, jnp.concatenate(slabs, 0))
            for a in range(3):
                at = QUARTER * (9 * a + 3 * (b + 1) + c + 1)
                block = part[QUARTER * a : QUARTER * (a + 1)]
                wide[at : at + QUARTER, :] = block[:, :128]
                for q in range(4):
                    start = SB + at - q
                    narrow[start : start + QUARTER, 32 * q : 32 * (q + 1)] = block[:, 128:]
    for t in range(8):
        for p in range(2):
            start = (270 * p + (135 * t) // 4 - x + 3) >> 2
            for y in range(2):
                blocks = []
                for n in range(UNIT):
                    if n < 9:
                        rows = pl.ds(start + 135 * y + n, ROUND, stride=270)
                        blocks.append(wide[rows, :])
                    else:
                        rows = pl.ds(SB + start + 135 * y + 4 * (n - 9), ROUND, stride=270)
                        blocks.append(narrow[rows, :])
                share = 8 * (2 * y + p) + t
                for n in range(0, UNIT, 2):
                    pair = jnp.concatenate(blocks[n : n + 2], 0).astype(BF16)
                    out[share, 8 * n : 8 * n + 16] = pair


def attn_sum_kernel(a1, a2, b1, b2, held, out, low, high, ends):
    out[:, : 8 * UNIT] = held[...]
    turned = jnp.concatenate([a1[...], a2[...]], 0).T
    b = jnp.concatenate([b1[...], b2[...]], 0)
    flat, heads = turned[:WIDTH], turned[WIDTH:]
    part = dot(flat, b[:, : 3 * 256])
    for k in range(3):
        low[WIDTH * k : WIDTH * (k + 1), :] = part[:, 256 * k : 256 * k + 128]
        high[WIDTH * k : WIDTH * (k + 1), :] = part[:, 256 * k + 128 : 256 * (k + 1)]
    part = dot(heads, b[:, 3 * 256 : 4 * 256])
    low[3 * WIDTH :, :] = part[:, :128]
    high[3 * WIDTH :, :] = part[:, 128:]
    tail = b[:, 1152:]
    first = lane_half(WIDTH)
    pairs = (dot(flat, b[:, 1024:1152]), jnp.where(first, dot(flat, tail), dot(heads, tail)))
    for k in range(4):
        plain = pairs[k // 2]
        rolled = pltpu.roll(plain, 64, 1)
        here, there = (plain, rolled) if k % 2 == 0 else (rolled, plain)
        ends[SB + WIDTH * k : SB + WIDTH * (k + 1), :64] = here[:, :64]
        at = SB + WIDTH * k - 5
        ends[at : at + WIDTH, 64:] = there[:, 64:]
    for share in range(32):
        blocks = []
        for e in range(5):
            one = 80 * (share // 8) + 10 * (share % 8) + e
            rows = pl.ds(one, ROUND, stride=320)
            more = pl.ds(one + 5, ROUND, stride=320)
            blocks += [low[rows, :], high[rows, :], low[more, :], high[more, :]]
            blocks.append(ends[pl.ds(SB + one, ROUND, stride=320), :])
        blocks.append(jnp.zeros((ROUND, 128), F32))
        for n in range(0, 26, 2):
            pair = jnp.concatenate(blocks[n : n + 2], 0).astype(BF16)
            at = 8 * (UNIT + n)
            out[share, at : at + 16] = pair


def gather_kernel(info, given, out, sums):
    def added(sources, rows):
        total = given[sources[0], rows].astype(F32)
        for n in sources[1:]:
            total += given[n, rows].astype(F32)
        return total

    count = 8 * UNIT
    for c in range(2):
        for n in range(GROUP):
            turn = (info[4] + n) & (GROUP - 1)
            sources = [8 * (2 * y + c) + GROUP * h + turn for y in range(2) for h in range(2)]
            at = count * (GROUP * c + n)
            sums[at : at + count, :] = added(sources, slice(0, count))
        sources = [8 * (2 * y + c) + t for y in range(2) for t in range(8)]
        at = 8 * (count + 25 * c)
        sums[at : at + 200, :] = added(sources, slice(count, count + 208))[:200]
    sums[8 * TOTALS :, :] = jnp.zeros((48, 128), F32)
    for z in range(ROUND):
        out[z] = sums[pl.ds(z, TOTALS + 6, stride=8), :].astype(BF16)


def passed_along(block, axis, distance):
    devices = range(lax.axis_size(axis))
    route = [(i - distance, i) for i in devices if i - distance in devices]
    return lax.ppermute(block, axis, route)


def swapped(block):
    return lax.ppermute(block, "win", [(i, i ^ 1) for i in range(lax.axis_size("win"))])


def exchanged(block, distance):
    return lax.ppermute(block, "tile", [(i, i ^ distance) for i in range(lax.axis_size("tile"))])


def local(frames_in, w_attn, conv_weight, fade, grad_out):
    position = lax.axis_index("win")
    tile = lax.axis_index("tile")
    core = position % 2
    last = position == lax.axis_size("win") - 1
    begin = (2 * position + (135 * tile) // 4) % GROUP
    info = jnp.stack([last, core, tile % GROUP, tile // GROUP, begin]).astype(jnp.int32)
    pad = ((0, 0), (0, 0), (0, 2), (0, 0))
    own = jnp.pad(frames_in, pad).reshape(OWN, WIDTH)
    gpad = jnp.pad(grad_out, pad)
    gout = gpad.reshape(OWN, WIDTH)
    gframes = jnp.pad(gpad[..., :CONV], ((0, 0), (0, 0), (0, 0), (0, 64)))
    gframes = gframes.reshape(OWN, 384)
    first = jnp.pad(gpad[0, ..., :CONV].reshape(16, CONV), ((0, 0), (0, CONV)))
    tail = passed_along(jnp.concatenate([own[:TAIL], first], 0), "win", -1)
    before = passed_along(gframes[OWN - 16 :], "win", 1)
    gframes = jnp.concatenate([before, gframes, tail[TAIL:, :384]], 0)
    pieces = [gframes] + [exchanged(gframes, d) for d in (1, 2, 3)]
    sides = gframes.reshape(STRIDE + 2, 2, 8, 384)
    sides = jnp.where(tile < GROUP, sides[:, 1], sides[:, 0]).reshape(SHARED // 2, 384)
    border = lax.ppermute(sides, "tile", [(GROUP - 1, GROUP), (GROUP, GROUP - 1)])

    qkv, probs, mine, branch, carried = call(
        forward_kernel,
        (
            shp((ALL, 3 * WIDTH), BF16),
            shp((HEADS, ALL, ALL), F32),
            shp((ALL, 2 * WIDTH), BF16),
            shp((OWN, WIDTH), F32),
            shp((TAIL + 16, WIDTH), BF16),
        ),
        specs=sm(2) + vm(3),
        us=4,
    )(info, fade, own, tail, w_attn)
    before = passed_along(carried, "win", 1)
    theirs = swapped(mine)
    back, gkeep, gaway, gedge = call(
        conv_back_kernel,
        (
            shp((OWN, CONV), F32),
            shp((GROUP * SHARED, 256), BF16),
            shp((GROUP * SHARED, 256), BF16),
            shp((SHARED // 2, 384), BF16),
        ),
        [pltpu.VMEM((9, 14 * 16, CONV), BF16), pltpu.VMEM((CONV, OWN), F32)],
        specs=sm(1) + vm(6),
        us=3,
    )(info, *pieces, border, conv_weight)
    gother = swapped(gaway)
    *acts, gmix, gown, gsend = call(
        mixed_kernel,
        (
            *[shp((OWN, 128), BF16)] * GROUP,
            shp((OWN, WIDTH), F32),
            shp((OWN, WIDTH), BF16),
            shp((TAIL, WIDTH), BF16),
        ),
        specs=sm(1) + vm(5),
        us=1,
    )(info, own, branch, before, back, gout)
    gedge, gown = lax.optimization_barrier((gedge, gown))
    gedge = exchanged(gedge, GROUP)
    gtail = passed_along(gsend, "win", -1)
    gtail, gedge, acts = lax.optimization_barrier((gtail, gedge, acts))
    acts = [acts[0]] + [exchanged(acts[d], d) for d in (1, 2, 3)]
    acts = jnp.concatenate(acts, 0)
    others = swapped(acts)
    eother = swapped(gedge)
    gqkv, keep, send = call(
        backward_kernel,
        (shp((ALL, 3 * WIDTH), BF16), shp((ALL, 1280), BF16), shp((ALL, 1280), BF16)),
        specs=sm(1) + vm(5),
        us=5,
    )(info, qkv, probs, gown, gtail, w_attn)
    other = swapped(send)
    total, gback = call(
        window_kernel,
        (shp((OWN, WIDTH), F32), shp((TAIL, WIDTH), BF16)),
        specs=vm(3),
        us=1,
    )(gqkv, w_attn, gmix)
    returned = passed_along(gback, "win", 1)
    shares = call(
        conv_sum_kernel,
        shp((32, 8 * UNIT, 128), BF16),
        [
            pltpu.VMEM((ROWS_C + 16, 128), F32),
            pltpu.VMEM((SB + ROWS_C + 24, 128), F32),
        ],
        specs=sm(1) + vm(6),
        us=4,
    )(info, acts, others, gkeep, gother, gedge, eother)
    shares = call(
        attn_sum_kernel,
        shp((32, 8 * BLOCKS, 128), BF16),
        [
            pltpu.VMEM((4 * WIDTH, 128), F32),
            pltpu.VMEM((4 * WIDTH, 128), F32),
            pltpu.VMEM((SB + 4 * WIDTH, 128), F32),
        ],
        specs=vm(5),
        us=4,
    )(mine, theirs, keep, other, shares)
    devices = lax.axis_size("win") * lax.axis_size("tile")
    planes = [[32 * z + n for n in range(32)] for z in range(ROUND)]
    lines = [[32 * z + n for z in range(ROUND)] for n in range(32)]
    both = ("win", "tile")
    shares = lax.all_to_all(shares, both, 0, 0, tiled=True, axis_index_groups=planes)
    shares = call(
        gather_kernel,
        shp((ROUND, TOTALS + 6, 128), BF16),
        [pltpu.VMEM((8 * TOTALS + 48, 128), F32)],
        specs=sm(1) + vm(1),
        us=1.5,
    )(info, shares)
    shares = lax.all_to_all(shares, both, 0, 0, tiled=True, axis_index_groups=lines)

    factor = 1.0 / math.sqrt(STRIDE * 12 * devices)
    sums = jnp.sum(shares.astype(F32), axis=0) * factor
    conv = sums[: 8 * UNIT].reshape(2, GROUP, UNIT, 128)
    big = conv[:, :, :9].transpose(1, 2, 0, 3).reshape(GROUP, 9, 256)
    small = conv[:, :, 9:].reshape(2, GROUP, UNIT, 32)[:, :, :9]
    small = small.transpose(1, 2, 0, 3).reshape(GROUP, 9, 64)
    conv = jnp.concatenate([big, small], -1)
    conv = conv.transpose(1, 0, 2).reshape(-1)
    grad_conv = lax.dynamic_slice(conv, (240 * tile % 320,), (10800,))
    attn = sums[8 * UNIT : TOTALS].reshape(2, 5, 5, 128)
    big = attn[:, :, :4].reshape(2, 5, 2, 2, 128).transpose(2, 1, 0, 3, 4).reshape(10, 512)
    small = attn[:, :, 4].reshape(2, 5, 2, 64).transpose(2, 1, 0, 3).reshape(10, 128)
    grad_attn = jnp.concatenate([big, small], -1).reshape(-1)

    total = jnp.concatenate([total[:TAIL] + returned.astype(F32), total[TAIL:]], 0)
    grad_x = total.astype(BF16).reshape(STRIDE, 2, 8, WIDTH)[:, :, :6]
    return (grad_x, grad_attn, grad_conv)


def solution(mesh):
    placed = (P("win", "tile", None, None), P(), P(), P("win", None), P("win", "tile", None, None))
    return jax.shard_map(
        local,
        mesh=mesh,
        in_specs=placed,
        out_specs=(P("win", "tile", None, None), P(("win", "tile")), P(("win", "tile"))),
        check_vma=False,
    )
```

```python
import functools
import math

import jax
import jax.numpy as jnp
from jax import lax
from jax.experimental import pallas as pl
from jax.experimental.pallas import tpu as pltpu
from jax.sharding import PartitionSpec as P

HEADS = 10
CONV = 320
WIN_LEN = 16
STRIDE = 12
OVER = 4
WIDTH = 640
PLACES = 16
OWN = STRIDE * PLACES
TAIL = OVER * PLACES
ALL = OWN + TAIL
UNIT = 12
BLOCKS = 38
ROUND = 8
TOTALS = 8 * UNIT + 2 * 25
GROUP = 4
QUARTER = CONV // GROUP
SHARED = (STRIDE + 2) * 16
SB = 8
F32 = jnp.float32
BF16 = jnp.bfloat16
ROWS_C = 27 * QUARTER

NN = (((1,), (0,)), ((), ()))
NT = (((1,), (1,)), ((), ()))
TN = (((0,), (0,)), ((), ()))


def dot(a, b, dims=NN):
    return lax.dot_general(a, b, dims, preferred_element_type=F32)


def call(kernel, outs, scratch=(), specs=None, out_specs=None, aliases=None, us=1.0):
    if out_specs is None:
        out_specs = tuple(vm(len(outs))) if isinstance(outs, tuple) else vm(1)[0]
    return pl.pallas_call(
        kernel,
        out_shape=outs,
        in_specs=specs,
        out_specs=out_specs,
        scratch_shapes=scratch,
        input_output_aliases=aliases or {},
        compiler_params=pltpu.CompilerParams(vmem_limit_bytes=16 << 20),
        cost_estimate=pl.CostEstimate(
            flops=int(us * 1e9), bytes_accessed=int(us * 3e6), transcendentals=0
        ),
    )


def vm(n):
    return [pl.BlockSpec(memory_space=pltpu.VMEM)] * n


def sm(n):
    return [pl.BlockSpec(memory_space=pltpu.SMEM)] * n


def shp(shape, dtype):
    return jax.ShapeDtypeStruct(shape, dtype)


def lane_half(rows):
    return lax.broadcasted_iota(jnp.int32, (rows, 128), 1) < 64


def forward_kernel(info, fade, own, tail, w, qkv, probs, mine, branch, carried):
    x = jnp.concatenate([own[...], tail[:TAIL]], 0)
    mine[:, :WIDTH] = x
    for k in range(3):
        qkv[:, WIDTH * k : WIDTH * (k + 1)] = dot(x, w[k]).astype(BF16)
    scale = 64 ** (-0.5)
    row = lax.broadcasted_iota(jnp.int32, (ALL, ALL), 0)
    col = lax.broadcasted_iota(jnp.int32, (ALL, ALL), 1)
    limit = ALL - TAIL * info[0]
    bias = jnp.where((((row ^ col) & (PLACES - 1)) == 0) & (col < limit), 0.0, -1e30)
    first = lane_half(ALL)
    for pair in range(HEADS // 2):
        at = 128 * pair
        q = qkv[:, at : at + 128]
        k = qkv[:, WIDTH + at : WIDTH + at + 128]
        v = qkv[:, 2 * WIDTH + at : 2 * WIDTH + at + 128]
        results = []
        for side in range(2):
            picked = jnp.where(first if side == 0 else ~first, q, jnp.zeros_like(q))
            scores = dot(picked, k, NT) * scale + bias
            expo = jnp.exp(scores - jnp.max(scores, axis=-1, keepdims=True))
            prob = expo * (1.0 / jnp.sum(expo, axis=-1, keepdims=True))
            probs[2 * pair + side] = prob
            results.append(dot(prob.astype(BF16), v))
        mine[:, WIDTH + at : WIDTH + at + 128] = jnp.where(first, results[0], results[1]).astype(BF16)
    out = dot(mine[:, WIDTH:], w[3])
    branch[...] = out[:OWN]
    lines = lax.broadcasted_iota(jnp.int32, (16, WIDTH), 0)
    table = jnp.zeros((16, WIDTH), F32)
    for t in range(OVER):
        frac = fade[0, t].astype(F32) / 16.0
        part = out[OWN + PLACES * t : OWN + PLACES * (t + 1)]
        carried[PLACES * t : PLACES * (t + 1)] = (frac * part).astype(BF16)
        table = jnp.where(lines == t, frac, table)
    carried[TAIL:] = table.astype(BF16)


def shifted(g, c):
    if c == 1:
        return jnp.concatenate([g[-1:], g[:-1]], 0)
    if c == -1:
        return jnp.concatenate([g[1:], g[:1]], 0)
    return g


def slab_of(g, b, c, frames, rows):
    width = g.shape[-1]
    lines = shifted(g, c).reshape(frames, 8 * (rows + 2), width)
    lines = lines[:, 8 * (1 - b) : 8 * (1 - b) + 8 * rows, :]
    return lines.astype(BF16).reshape(frames * 8 * rows, width)


def conv_back_kernel(info, g0, g1, g2, g3, edge, w, out, keep, send, away, slabs, acc):
    x, upper = info[2], info[3]
    lower = info[1] == 0
    row = (x ^ (GROUP - 1)) * (1 - upper) + x * upper
    border = jnp.zeros((SHARED, 384), BF16)
    for d, g in enumerate((g0, g1, g2, g3)):
        at = slice(SHARED * d, SHARED * (d + 1))
        left, right, end = g[:, :128], g[:, 128:256], g[:, 256:]
        keep[at, :128] = jnp.where(lower, left, right)
        send[at, :128] = jnp.where(lower, right, left)
        keep[at, 128:] = end
        send[at, 128:] = end
        border = jnp.where(row == d, g[...], border)
    border = border.astype(F32).reshape(STRIDE + 2, 16, 384)
    border = jnp.where(upper == 0, border[:, 8:], border[:, :8])
    away[...] = border.reshape(SHARED // 2, 384).astype(BF16)
    border = edge[...].astype(F32).reshape(STRIDE + 2, 8, 384)
    parts = [g[...].astype(F32).reshape(STRIDE + 2, 16, 384) for g in (g0, g1, g2, g3)]

    def row_of(n, half):
        return parts[n][:, 8 * half : 8 * half + 8]

    blank = jnp.zeros_like(border)
    low = jnp.where(x == 0, jnp.where(upper == 1, border, blank), row_of(1, 1))
    low = jnp.where(x == 2, row_of(3, 1), low)
    high = jnp.where(x == 3, jnp.where(upper == 1, blank, border), row_of(1, 0))
    high = jnp.where(x == 1, row_of(3, 0), high)
    lines = jnp.concatenate([low, parts[0], high], 1).reshape((STRIDE + 2) * 32, 384)
    lines = lines[:, :CONV]
    for b in (-1, 0, 1):
        for c in (-1, 0, 1):
            slabs[3 * (b + 1) + c + 1] = slab_of(lines, b, c, STRIDE + 2, 2)
    for a in (-1, 0, 1):
        for j in range(9):
            part = slabs[j, 16 * (1 - a) : 16 * (1 - a) + OWN, :]
            term = dot(w[9 * (a + 1) + j], part, NT)
            if a == -1 and j == 0:
                acc[...] = term
            else:
                acc[...] += term
    out[...] = acc[...].T


def mixed_kernel(
    info, own, branch, before, back, gout, act0, act1, act2, act3, gmix, gown, gsend
):
    lines = lax.broadcasted_iota(jnp.int32, (OWN, 1), 0)
    inside = (lines & 7) < 6
    prev = jnp.zeros((TAIL, 1), F32)
    for t in range(OVER):
        value = before[TAIL + t : TAIL + t + 1, 0:1].astype(F32)
        prev = jnp.where((lines[:TAIL] >> 4) == t, value, prev)
    head = 1.0 - prev
    top = head * branch[:TAIL] + before[:TAIL].astype(F32)
    mixed = own[...].astype(F32) + jnp.concatenate([top, branch[TAIL:]], 0)
    conv_in = mixed[:, :CONV]
    sig = 1.0 / (1.0 + jnp.exp(-conv_in))
    value = (conv_in * sig).astype(BF16)
    channel = lax.broadcasted_iota(jnp.int32, (CONV, 128), 0)
    column = lax.broadcasted_iota(jnp.int32, (CONV, 128), 1)
    for d in range(GROUP):
        wanted = GROUP * column + (info[2] ^ d)
        pick = jnp.where((channel == wanted) & (column < QUARTER), 1.0, 0.0).astype(BF16)
        (act0, act1, act2, act3)[d][...] = dot(value, pick).astype(BF16)
    slope = sig * (1.0 + conv_in * (1.0 - sig))
    extra = jnp.where(inside, back[...] * slope, 0.0)
    gmix[...] = gout[...].astype(F32)
    gmix[:, :CONV] += extra
    total = gmix[...]
    beta = jnp.concatenate([head, jnp.ones((OWN - TAIL, 1), F32)], 0)
    gown[...] = (beta * total).astype(BF16)
    gsend[...] = (prev * total[:TAIL]).astype(BF16)


def backward_kernel(info, qkv, probs, gown, gtail, w, gqkv, keep, send):
    scale = 64 ** (-0.5)
    gb = jnp.concatenate([gown[...], gtail[...]], 0)
    gh = dot(gb, w[3], NT).astype(BF16)
    first = lane_half(ALL)
    zero = jnp.zeros((ALL, 128), BF16)
    for pair in range(HEADS // 2):
        at = 128 * pair
        q = qkv[:, at : at + 128]
        k = qkv[:, WIDTH + at : WIDTH + at + 128]
        v = qkv[:, 2 * WIDTH + at : 2 * WIDTH + at + 128]
        g = gh[:, at : at + 128]
        results = []
        for side in range(2):
            prob = probs[2 * pair + side]
            gp = dot(jnp.where(first if side == 0 else ~first, g, zero), v, NT)
            inner = jnp.sum(prob * gp, axis=-1, keepdims=True)
            gs = (prob * (gp - inner) * scale).astype(BF16)
            results.append((dot(gs, k), dot(gs, q, TN), dot(prob.astype(BF16), g, TN)))
        for n in range(3):
            picked = jnp.where(first, results[0][n], results[1][n])
            gqkv[:, WIDTH * n + at : WIDTH * n + at + 128] = picked.astype(BF16)
    lower = info[1] == 0
    ends = []
    for n in range(4):
        part = gqkv[:, WIDTH * n : WIDTH * (n + 1)] if n < 3 else gb
        low, high = part[:, :256], part[:, 256:512]
        keep[:, 256 * n : 256 * (n + 1)] = jnp.where(lower, low, high)
        send[:, 256 * n : 256 * (n + 1)] = jnp.where(lower, high, low)
        ends.append(part[:, 512:])
    for n in range(2):
        one, two = ends[2 * n], ends[2 * n + 1]
        low = jnp.concatenate([one[:, :64], two[:, :64]], 1)
        high = jnp.concatenate([one[:, 64:], two[:, 64:]], 1)
        keep[:, 1024 + 128 * n : 1152 + 128 * n] = jnp.where(lower, low, high)
        send[:, 1024 + 128 * n : 1152 + 128 * n] = jnp.where(lower, high, low)


def window_kernel(gqkv, w, gmix, total, back):
    acc = dot(gqkv[:, :WIDTH], w[0], NT)
    acc += dot(gqkv[:, WIDTH : 2 * WIDTH], w[1], NT)
    acc += dot(gqkv[:, 2 * WIDTH :], w[2], NT)
    total[...] = gmix[...] + acc[:OWN]
    back[...] = acc[OWN:].astype(BF16)


def conv_sum_kernel(info, a1, a2, g1, g2, e1, e2, out, wide, narrow, stage, sem):
    x, upper = info[2], info[3]
    frames = STRIDE + 2
    half = CONV // 2
    left = [[], [], []]
    lines = []
    gap = jnp.zeros((QUARTER, 64), BF16)
    for act, g, e in ((a1, g1, e1), (a2, g2, e2)):
        places = [pl.ds(pl.multiple_of(OWN * (x ^ n), 16), OWN) for n in range(GROUP)]
        rows = [act[at, :].reshape(STRIDE, 1, 16, 128) for at in places]
        turned = jnp.concatenate(rows, 1).reshape(STRIDE * 64, 128).T[:QUARTER]
        left[0] += [gap, gap, turned]
        left[1] += [gap, turned, gap]
        left[2] += [turned, gap, gap]

        def cut(value):
            value = value.astype(F32)
            end = value[:, 128:]
            end = jnp.where(info[1] == 0, end, pltpu.roll(end, 96, 1))[:, :32]
            return jnp.concatenate([value[:, :128], end], 1).reshape(frames, -1, half)

        border = e[...]
        start = jnp.where(info[1] == 0, border[:, :128], border[:, 128:256])
        border = cut(jnp.concatenate([start, border[:, 256:]], 1))
        before = jnp.where(upper == 1, border, 0.0)
        after = jnp.where(upper == 1, 0.0, border)
        places = [pl.ds(pl.multiple_of(SHARED * (x ^ n), 16), SHARED) for n in range(GROUP)]
        inner = [cut(g[at, :]) for at in places]
        lines.append(jnp.concatenate([before] + inner + [after], 1).reshape(frames * 80, half))
    left = jnp.concatenate([jnp.concatenate(line, 1) for line in left], 0)
    wide[ROWS_C:, :] = jnp.zeros((16, 128), F32)
    narrow[...] = jnp.zeros(narrow.shape, F32)
    for b in (-1, 0, 1):
        for c in (-1, 0, 1):
            slabs = [slab_of(line, b, c, frames, 8) for line in lines]
            part = dot(left, jnp.concatenate(slabs, 0))
            for a in range(3):
                at = QUARTER * (9 * a + 3 * (b + 1) + c + 1)
                block = part[QUARTER * a : QUARTER * (a + 1)]
                wide[at : at + QUARTER, :] = block[:, :128]
                for q in range(4):
                    start = SB + at - q
                    narrow[start : start + QUARTER, 32 * q : 32 * (q + 1)] = block[:, 128:]
    for t in range(8):
        for p in range(2):
            start = (270 * p + (135 * t) // 4 - x + 3) >> 2
            for y in range(2):
                blocks = []
                for n in range(UNIT):
                    if n < 9:
                        rows = pl.ds(start + 135 * y + n, ROUND, stride=270)
                        blocks.append(wide[rows, :])
                    else:
                        rows = pl.ds(SB + start + 135 * y + 4 * (n - 9), ROUND, stride=270)
                        blocks.append(narrow[rows, :])
                share = 8 * (2 * y + p) + t
                for n in range(0, UNIT, 2):
                    pair = jnp.concatenate(blocks[n : n + 2], 0).astype(BF16)
                    stage[share, 8 * n : 8 * n + 16] = pair
    copy = pltpu.make_async_copy(stage, out.at[:, 0 : 8 * UNIT], sem)
    copy.start()
    copy.wait()


def attn_sum_kernel(a1, a2, b1, b2, held, out, low, high, ends, stage, sem):
    del held
    turned = jnp.concatenate([a1[...], a2[...]], 0).T
    b = jnp.concatenate([b1[...], b2[...]], 0)
    flat, heads = turned[:WIDTH], turned[WIDTH:]
    part = dot(flat, b[:, : 3 * 256])
    for k in range(3):
        low[WIDTH * k : WIDTH * (k + 1), :] = part[:, 256 * k : 256 * k + 128]
        high[WIDTH * k : WIDTH * (k + 1), :] = part[:, 256 * k + 128 : 256 * (k + 1)]
    part = dot(heads, b[:, 3 * 256 : 4 * 256])
    low[3 * WIDTH :, :] = part[:, :128]
    high[3 * WIDTH :, :] = part[:, 128:]
    tail = b[:, 1152:]
    first = lane_half(WIDTH)
    pairs = (dot(flat, b[:, 1024:1152]), jnp.where(first, dot(flat, tail), dot(heads, tail)))
    for k in range(4):
        plain = pairs[k // 2]
        rolled = pltpu.roll(plain, 64, 1)
        here, there = (plain, rolled) if k % 2 == 0 else (rolled, plain)
        ends[SB + WIDTH * k : SB + WIDTH * (k + 1), :64] = here[:, :64]
        at = SB + WIDTH * k - 5
        ends[at : at + WIDTH, 64:] = there[:, 64:]
    for share in range(32):
        blocks = []
        for e in range(5):
            one = 80 * (share // 8) + 10 * (share % 8) + e
            rows = pl.ds(one, ROUND, stride=320)
            more = pl.ds(one + 5, ROUND, stride=320)
            blocks += [low[rows, :], high[rows, :], low[more, :], high[more, :]]
            blocks.append(ends[pl.ds(SB + one, ROUND, stride=320), :])
        blocks.append(jnp.zeros((ROUND, 128), F32))
        for n in range(0, 26, 2):
            pair = jnp.concatenate(blocks[n : n + 2], 0).astype(BF16)
            stage[share, 8 * n : 8 * n + 16] = pair
    copy = pltpu.make_async_copy(stage, out.at[:, 8 * UNIT :], sem)
    copy.start()
    copy.wait()


def gather_kernel(given, out, sums):
    def added(sources, rows):
        total = given[sources[0], rows].astype(F32)
        for n in sources[1:]:
            total += given[n, rows].astype(F32)
        return total

    count = 8 * UNIT
    for c in range(2):
        for n in range(GROUP):
            sources = [8 * (2 * y + c) + GROUP * h + n for y in range(2) for h in range(2)]
            at = count * (GROUP * c + n)
            sums[at : at + count, :] = added(sources, slice(0, count))
        sources = [8 * (2 * y + c) + t for y in range(2) for t in range(8)]
        at = 8 * (count + 25 * c)
        sums[at : at + 200, :] = added(sources, slice(count, count + 208))[:200]
    sums[8 * TOTALS :, :] = jnp.zeros((48, 128), F32)
    for z in range(ROUND):
        out[z] = sums[pl.ds(z, TOTALS + 6, stride=8), :].astype(BF16)


def passed_along(block, axis, distance):
    devices = range(lax.axis_size(axis))
    route = [(i - distance, i) for i in devices if i - distance in devices]
    return lax.ppermute(block, axis, route)


def swapped(block):
    return lax.ppermute(block, "win", [(i, i ^ 1) for i in range(lax.axis_size("win"))])


def exchanged(block, distance):
    return lax.ppermute(block, "tile", [(i, i ^ distance) for i in range(lax.axis_size("tile"))])


def local(frames_in, w_attn, conv_weight, fade, grad_out):
    position = lax.axis_index("win")
    tile = lax.axis_index("tile")
    core = position % 2
    last = position == lax.axis_size("win") - 1
    info = jnp.stack([last, core, tile % GROUP, tile // GROUP]).astype(jnp.int32)
    pad = ((0, 0), (0, 0), (0, 2), (0, 0))
    own = jnp.pad(frames_in, pad).reshape(OWN, WIDTH)
    gpad = jnp.pad(grad_out, pad)
    gout = gpad.reshape(OWN, WIDTH)
    gframes = jnp.pad(gpad[..., :CONV], ((0, 0), (0, 0), (0, 0), (0, 64)))
    gframes = gframes.reshape(OWN, 384)
    first = jnp.pad(gpad[0, ..., :CONV].reshape(16, CONV), ((0, 0), (0, CONV)))
    tail = passed_along(jnp.concatenate([own[:TAIL], first], 0), "win", -1)
    before = passed_along(gframes[OWN - 16 :], "win", 1)
    gframes = jnp.concatenate([before, gframes, tail[TAIL:, :384]], 0)
    pieces = [gframes] + [exchanged(gframes, d) for d in (1, 2, 3)]
    sides = gframes.reshape(STRIDE + 2, 2, 8, 384)
    sides = jnp.where(tile < GROUP, sides[:, 1], sides[:, 0]).reshape(SHARED // 2, 384)
    border = lax.ppermute(sides, "tile", [(GROUP - 1, GROUP), (GROUP, GROUP - 1)])

    qkv, probs, mine, branch, carried = call(
        forward_kernel,
        (
            shp((ALL, 3 * WIDTH), BF16),
            shp((HEADS, ALL, ALL), F32),
            shp((ALL, 2 * WIDTH), BF16),
            shp((OWN, WIDTH), F32),
            shp((TAIL + 16, WIDTH), BF16),
        ),
        specs=sm(2) + vm(3),
        us=4,
    )(info, fade, own, tail, w_attn)
    before = passed_along(carried, "win", 1)
    theirs = swapped(mine)
    back, gkeep, gaway, gedge = call(
        conv_back_kernel,
        (
            shp((OWN, CONV), F32),
            shp((GROUP * SHARED, 256), BF16),
            shp((GROUP * SHARED, 256), BF16),
            shp((SHARED // 2, 384), BF16),
        ),
        [pltpu.VMEM((9, 14 * 16, CONV), BF16), pltpu.VMEM((CONV, OWN), F32)],
        specs=sm(1) + vm(6),
        us=3,
    )(info, *pieces, border, conv_weight)
    gother = swapped(gaway)
    *acts, gmix, gown, gsend = call(
        mixed_kernel,
        (
            *[shp((OWN, 128), BF16)] * GROUP,
            shp((OWN, WIDTH), F32),
            shp((OWN, WIDTH), BF16),
            shp((TAIL, WIDTH), BF16),
        ),
        specs=sm(1) + vm(5),
        us=1,
    )(info, own, branch, before, back, gout)
    gedge, gown = lax.optimization_barrier((gedge, gown))
    gedge = exchanged(gedge, GROUP)
    gtail = passed_along(gsend, "win", -1)
    gtail, gedge, acts = lax.optimization_barrier((gtail, gedge, acts))
    acts = [acts[0]] + [exchanged(acts[d], d) for d in (1, 2, 3)]
    acts = jnp.concatenate(acts, 0)
    others = swapped(acts)
    eother = swapped(gedge)
    gqkv, keep, send = call(
        backward_kernel,
        (shp((ALL, 3 * WIDTH), BF16), shp((ALL, 1280), BF16), shp((ALL, 1280), BF16)),
        specs=sm(1) + vm(5),
        us=5,
    )(info, qkv, probs, gown, gtail, w_attn)
    other = swapped(send)
    total, gback = call(
        window_kernel,
        (shp((OWN, WIDTH), F32), shp((TAIL, WIDTH), BF16)),
        specs=vm(3),
        us=1,
    )(gqkv, w_attn, gmix)
    gkeep, gback = lax.optimization_barrier((gkeep, gback))
    returned = passed_along(gback, "win", 1)
    anyspace = pl.BlockSpec(memory_space=pl.ANY)
    shares = call(
        conv_sum_kernel,
        shp((32, 8 * BLOCKS, 128), BF16),
        [
            pltpu.VMEM((ROWS_C + 16, 128), F32),
            pltpu.VMEM((SB + ROWS_C + 24, 128), F32),
            pltpu.VMEM((32, 8 * UNIT, 128), BF16),
            pltpu.SemaphoreType.DMA,
        ],
        specs=sm(1) + vm(6),
        out_specs=anyspace,
        us=4,
    )(info, acts, others, gkeep, gother, gedge, eother)
    shares = call(
        attn_sum_kernel,
        shp((32, 8 * BLOCKS, 128), BF16),
        [
            pltpu.VMEM((4 * WIDTH, 128), F32),
            pltpu.VMEM((4 * WIDTH, 128), F32),
            pltpu.VMEM((SB + 4 * WIDTH, 128), F32),
            pltpu.VMEM((32, 8 * (BLOCKS - UNIT), 128), BF16),
            pltpu.SemaphoreType.DMA,
        ],
        specs=vm(4) + [anyspace],
        out_specs=anyspace,
        aliases={4: 0},
        us=4,
    )(mine, theirs, keep, other, shares)
    devices = lax.axis_size("win") * lax.axis_size("tile")
    planes = [[32 * z + n for n in range(32)] for z in range(ROUND)]
    lines = [[32 * z + n for z in range(ROUND)] for n in range(32)]
    both = ("win", "tile")
    shares = lax.all_to_all(shares, both, 0, 0, tiled=True, axis_index_groups=planes)
    shares = call(
        gather_kernel,
        shp((ROUND, TOTALS + 6, 128), BF16),
        [pltpu.VMEM((8 * TOTALS + 48, 128), F32)],
        specs=vm(1),
        us=1.5,
    )(shares)
    shares = lax.all_to_all(shares, both, 0, 0, tiled=True, axis_index_groups=lines)

    factor = 1.0 / math.sqrt(STRIDE * 12 * devices)
    sums = jnp.sum(shares.astype(F32), axis=0) * factor
    conv = sums[: 8 * UNIT].reshape(2, GROUP, UNIT, 128)
    big = conv[:, :, :9].transpose(1, 2, 0, 3).reshape(GROUP, 9, 256)
    small = conv[:, :, 9:].reshape(2, GROUP, UNIT, 32)[:, :, :9]
    small = small.transpose(1, 2, 0, 3).reshape(GROUP, 9, 64)
    conv = jnp.concatenate([big, small], -1)
    begin = (2 * position + (135 * tile) // 4) % GROUP
    conv = lax.dynamic_slice(jnp.concatenate([conv, conv], 0), (begin, 0, 0), (GROUP, 9, CONV))
    conv = conv.transpose(1, 0, 2).reshape(-1)
    grad_conv = lax.dynamic_slice(conv, (240 * tile % 320,), (10800,))
    attn = sums[8 * UNIT : TOTALS].reshape(2, 5, 5, 128)
    big = attn[:, :, :4].reshape(2, 5, 2, 2, 128).transpose(2, 1, 0, 3, 4).reshape(10, 512)
    small = attn[:, :, 4].reshape(2, 5, 2, 64).transpose(2, 1, 0, 3).reshape(10, 128)
    grad_attn = jnp.concatenate([big, small], -1).reshape(-1)

    total = jnp.concatenate([total[:TAIL] + returned.astype(F32), total[TAIL:]], 0)
    grad_x = total.astype(BF16).reshape(STRIDE, 2, 8, WIDTH)[:, :, :6]
    return (grad_x, grad_attn, grad_conv)


def solution(mesh):
    placed = (P("win", "tile", None, None), P(), P(), P("win", None), P("win", "tile", None, None))
    return jax.shard_map(
        local,
        mesh=mesh,
        in_specs=placed,
        out_specs=(P("win", "tile", None, None), P(("win", "tile")), P(("win", "tile"))),
        check_vma=False,
    )
```
